256 devices in a mesh: dp: 16 (over z, y_lo), ctx: 16 (over x, y_hi, core).
Axes of the slice: x: 4, y: 4 (y_hi: 2, y_lo: 2; y = y_hi * 2 + y_lo), z: 8, core: 2. Of those that a mesh axis runs over, the one named last changes fastest.
Arguments:
- layer_input: bfloat16 [16, 4096, 8192], P('dp', 'ctx'), may hold values from -0.078125 to 0.078125
- query_rows: bfloat16 [16, 4096, 1024], P('dp', 'ctx'), may hold values from -6 to 6
- key_rows: bfloat16 [16, 4096, 128], P('dp', 'ctx'), may hold values from -6 to 6
- value_rows: bfloat16 [16, 4096, 128], P('dp', 'ctx'), may hold values from -6 to 6
- attn_out: bfloat16 [16, 4096, 1024], P('dp', 'ctx'), may hold values from -6 to 6
- d_attn: bfloat16 [16, 4096, 1024], P('dp', 'ctx'), may hold values from -6 to 6
- log_sum_exp: float32 [16, 8, 4096], P('dp', None, 'ctx')
- block_order: int32 [32], replicated, may hold values from 0 to 31, as said below
Outputs:
- d_query: bfloat16 [16, 4096, 1024], P('dp', 'ctx')
- d_weight: float32 [8192, 256], P(('dp', 'ctx'))
The draws below stay inside these ranges and needn't reach their ends.
Inputs may be any that keep to these rules, and one draw needn't show every extreme that they name: `block_order`: each value appears exactly once.
All inputs are finite; a program needn't handle non-finite values.
Results may differ from the reference program's by a relative error of at most 0.0051.
Values may be sent and summed in bfloat16 or wider, within the bound.
No kernel may reach another device: no remote copies, remote signals or barrier semaphores. Data moves between devices by JAX's collectives and lax.ppermute only.
A program may use at most 64 MiB of HBM per device.

```python
import jax
import jax.numpy as jnp
from jax import lax

D = 8192
H = 8
DH = 128
TOK_DEV = 256
SEQ = 4096
BATCH = 16


def shared_order(key):
    return jax.random.permutation(jax.random.fold_in(key, 11), 2 * (SEQ // TOK_DEV)).astype(jnp.int32)


def draw_block_order(key, part):
    return shared_order(key)


def draw_log_sum_exp(key, part):
    order = shared_order(key)
    half = TOK_DEV // 2
    index = jnp.arange(SEQ, dtype=jnp.int32)
    positions = order[index // half] * half + index % half
    base = jnp.log(positions.astype(jnp.float32) + 1.0) + 0.5
    noise_key = jax.random.fold_in(key, 23)
    noise = jax.random.uniform(noise_key, (BATCH, H, SEQ), jnp.float32, -1.0, 1.0)
    return base[None, None, :] + noise


def strengthened(values, key, source, target, blocks, factor):
    owner, partner = [(jnp.arange(values.shape[position]) // (values.shape[position] // blocks)).reshape([-1 if axis == position else 1 for axis in range(values.ndim)]) for position in (source, target)]
    chosen = jax.random.permutation(key, blocks)[partner]
    strong = (owner == chosen) | (owner == (partner + blocks // 2) % blocks)
    return jnp.where(strong, factor * values, values)


def block_levels(rng, shape, split, low, largest):
    def one(axis_at, shards_of):
        steps = jax.random.uniform(jax.random.fold_in(jax.random.fold_in(rng, 6), axis_at), (shards_of,), jnp.float32, low / len(split), largest / len(split))
        return jnp.repeat(jnp.exp(steps), shape[axis_at] // shards_of).reshape((-1,) + (1,) * (len(shape) - axis_at - 1))

    loudness = one(*split[0])
    for cut in split[1:]:
        loudness = loudness * one(*cut)
    return loudness


def gaussian(rng, dims, spread, bound, cuts=(), kind=jnp.bfloat16):
    result = jax.random.normal(rng, dims, jnp.float32) * spread
    if len(cuts) > 0:
        result = block_levels(rng, dims, cuts, -0.22, 0.18) * result
    return jnp.clip(result, min=-bound, max=bound).astype(kind)


def gaussian_with(stream_key, extent, deviation, limit, shards, heavy, kind=jnp.bfloat16):
    entries = deviation * jax.random.normal(stream_key, extent, jnp.float32)
    if shards:
        entries = entries * block_levels(stream_key, extent, shards, -0.22, 0.18)
    return jnp.clip(strengthened(entries, jax.random.fold_in(stream_key, 3), *heavy), -limit, limit).astype(kind)


def setup_inputs(seed: int = 0) -> dict:
    streams_of = jax.random.split(jax.random.key(seed), 9)
    return {
        "layer_input": gaussian_with(streams_of[0], (BATCH, SEQ, D), 0.01, 0.078125, ((0, 16), (1, 16)), (1, 2, 16, 2.0)),
        "query_rows": gaussian(streams_of[1], (BATCH, SEQ, H * DH), 1.0, 6.0, ((0, 16), (1, 16))),
        "key_rows": gaussian(streams_of[2], (BATCH, SEQ, DH), 1.0, 6.0, ((0, 16), (1, 16))),
        "value_rows": gaussian(streams_of[3], (BATCH, SEQ, DH), 1.0, 6.0, ((0, 16), (1, 16))),
        "attn_out": gaussian(streams_of[4], (BATCH, SEQ, H * DH), 1.0, 6.0, ((0, 16), (1, 16))),
        "d_attn": gaussian(streams_of[5], (BATCH, SEQ, H * DH), 1.0, 6.0, ((0, 16), (1, 16))),
        "log_sum_exp": draw_log_sum_exp(jax.random.fold_in(streams_of[8], 71), 0),
        "block_order": draw_block_order(jax.random.fold_in(streams_of[8], 71), 0),
    }


def reference(layer_input, query_rows, key_rows, value_rows, attn_out, d_attn, log_sum_exp, block_order):
    half = TOK_DEV // 2
    index = jnp.arange(SEQ, dtype=jnp.int32)
    positions = block_order[index // half].astype(jnp.int32) * half + index % half
    visible = positions[:, None] >= positions[None, :]
    scale = DH ** -0.5

    def single(item):
        q_seq, k_seq, v_seq, out_seq, grad_seq, stats = item
        queries = q_seq.reshape(SEQ, H, DH).astype(jnp.float32)
        grad_out = grad_seq.reshape(SEQ, H, DH).astype(jnp.float32)
        saved = out_seq.reshape(SEQ, H, DH).astype(jnp.float32)
        keys = k_seq.astype(jnp.float32)
        values = v_seq.astype(jnp.float32)
        delta = jnp.sum(grad_out * saved, axis=2).T
        score = jnp.einsum("rhd,sd->hrs", queries, keys) * scale
        prob = jnp.where(visible[None], jnp.exp(score - stats[:, :, None]), jnp.float32(0.0))
        prob_b = lax.optimization_barrier(prob.astype(jnp.bfloat16)).astype(jnp.float32)
        d_value = jnp.einsum("hrs,rhd->sd", prob_b, grad_out)
        d_prob = jnp.einsum("rhd,sd->hrs", grad_out, values)
        d_score = prob * (d_prob - delta[:, :, None])
        d_score = lax.optimization_barrier(d_score.astype(jnp.bfloat16)).astype(jnp.float32)
        d_query = jnp.einsum("hrs,sd->rhd", d_score, keys) * scale
        d_key = jnp.einsum("hrs,rhd->sd", d_score, queries) * scale
        d_kv = jnp.concatenate([d_key, d_value], axis=1).astype(jnp.bfloat16)
        return d_query.reshape(SEQ, H * DH).astype(jnp.bfloat16), d_kv

    d_query, d_kv = lax.map(single, (query_rows, key_rows, value_rows, attn_out, d_attn, log_sum_exp))
    flat_inputs = layer_input.reshape(BATCH * SEQ, D)
    flat_grads = d_kv.reshape(BATCH * SEQ, 2 * DH)
    d_weight = jnp.dot(flat_inputs.T, flat_grads, preferred_element_type=jnp.float32)
    return d_query, d_weight
```

```python
import functools
import math

import jax
import jax.numpy as jnp
from jax import lax
from jax.experimental import pallas as pl
from jax.experimental.pallas import tpu as pltpu
from jax.sharding import PartitionSpec as P

F32 = jnp.float32
BF16 = jnp.bfloat16
BLK = 128
H = 8
Z, YL, X, YH, C = 8, 2, 4, 2, 2
CHUNK = 4
VMEM_LIMIT = 48 * 1024 * 1024


def coords(i):
    return (i // 32, i // 16 % 2, i // 4 % 4, i // 2 % 2, i % 2)


def index_of(z, yl, x, yh, c):
    return (((z * YL + yl) * X + x) * YH + yh) * C + c


def fetch(value, shift):
    pairs = [(index_of(*shift(*coords(i))), i) for i in range(Z * YL * X * YH * C)]
    return lax.ppermute(value, ("dp", "ctx"), pairs)


def swap_core(z, yl, x, yh, c):
    return (z, yl, x, yh, 1 - c)


def by_ctx(dx, dyh):
    return lambda z, yl, x, yh, c: (z, yl, (x + dx) % X, yh ^ dyh, c)


def by_x(k):
    return lambda z, yl, x, yh, c: (z, yl, (x + k) % X, yh, c)


def by_y(k):
    def shift(z, yl, x, yh, c):
        y = (2 * yh + yl + k) % 4
        return (z, y % 2, x, y // 2, c)

    return shift


def by_z(bit):
    return lambda z, yl, x, yh, c: (z ^ bit, yl, x, yh, c)


OFFSETS = [(dx, dyh) for dyh in range(YH) for dx in range(X)]


def vmem():
    return pl.BlockSpec(memory_space=pltpu.VMEM)


def smem():
    return pl.BlockSpec(memory_space=pltpu.SMEM)


def prep_kernel(me, x_ref, out_ref, grad_ref, lse_ref, mine_ref, other_ref, stats_ref):
    even = me[0] == 0
    for u in range(8):
        tile = x_ref[:, u * BLK : (u + 1) * BLK].T
        for yh in range(YH):
            first = tile[yh * 64 : yh * 64 + 32]
            second = tile[yh * 64 + 32 : yh * 64 + 64]
            at = slice(u * 64 + yh * 32, u * 64 + yh * 32 + 32)

            @pl.when(even)
            def _():
                mine_ref[at, :] = first
                other_ref[at, :] = second

            @pl.when(jnp.logical_not(even))
            def _():
                mine_ref[at, :] = second
                other_ref[at, :] = first

    @pl.when(pl.program_id(0) == 0)
    def _():
        stats_ref[...] = jnp.zeros_like(stats_ref)
        for h in range(H):
            cols = slice(h * BLK, (h + 1) * BLK)
            product = out_ref[:, cols].astype(F32) * grad_ref[:, cols].astype(F32)
            delta = jnp.sum(product.T, axis=0, keepdims=True)
            lse2 = lse_ref[h : h + 1, :] * math.log2(math.e)
            for i in range(2):
                rows = slice(i * BLK, (i + 1) * BLK)
                stats_ref[i : i + 1, cols] = lse2[:, rows]
                stats_ref[2 + i : 3 + i, cols] = delta[:, rows]


def prep(me, layer, saved, grad, lse):
    whole = lambda shape: pl.BlockSpec(shape, lambda z: (0,) * len(shape))
    return pl.pallas_call(
        prep_kernel,
        grid=(Z,),
        out_shape=(
            jax.ShapeDtypeStruct((4096, 256), BF16),
            jax.ShapeDtypeStruct((4096, 256), BF16),
            jax.ShapeDtypeStruct((8, H * BLK), F32),
        ),
        in_specs=[
            smem(),
            pl.BlockSpec((256, 1024), lambda z: (0, z)),
            whole((256, H * BLK)),
            whole((256, H * BLK)),
            whole((H, 256)),
        ],
        out_specs=(
            pl.BlockSpec((512, 256), lambda z: (z, 0)),
            pl.BlockSpec((512, 256), lambda z: (z, 0)),
            whole((8, H * BLK)),
        ),
        compiler_params=pltpu.CompilerParams(vmem_limit_bytes=VMEM_LIMIT),
        cost_estimate=pl.CostEstimate(flops=10**7, bytes_accessed=10 * 2**20, transcendentals=0),
        name="prep",
    )(me, layer, saved, grad, lse)


NQ, NK = 4, 16


def attn_kernel(meta, *refs):
    q_in, g_in, s_in = refs[0:2], refs[2:4], refs[4:6]
    kv_in = refs[6:14]
    dq_own, dq_other = refs[14:16]
    dkv_out = refs[16:24]
    q_all, g_all, qt, gt, kv, kt, dqt, dkv, stats = refs[24:]
    rows_all = H * BLK
    scale = BLK**-0.5
    factor = scale * math.log2(math.e)
    dkv[...] = jnp.zeros_like(dkv)
    for side in range(2):
        for i in range(2):
            n = 2 * side + i
            rows = slice(i * BLK, (i + 1) * BLK)
            q_all[n] = q_in[side][rows, :]
            g_all[n] = g_in[side][rows, :]
            stats[n : n + 1, :] = s_in[side][i : i + 1, :]
            stats[NQ + n : NQ + n + 1, :] = s_in[side][2 + i : 3 + i, :]

    def turn(n, carry):
        for h in range(H):
            cols = slice(h * BLK, (h + 1) * BLK)
            qt[n, :, cols] = q_all[n, :, cols].T
            gt[n, :, cols] = g_all[n, :, cols].T
        return carry

    lax.fori_loop(0, NQ, turn, 0)
    for b in range(8):
        for i in range(2):
            block = kv_in[b][i * BLK : (i + 1) * BLK, :]
            kv[2 * b + i] = block
            kt[2 * b + i] = block[:, :BLK].T

    keys = CHUNK * BLK

    def chunk(i, j, masked):
        at = [meta[j * CHUNK + n] for n in range(CHUNK)]
        kb = jnp.concatenate([kv[a, :, :BLK] for a in at], 0)
        vb = jnp.concatenate([kv[a, :, BLK:] for a in at], 0)
        ktb = jnp.concatenate([kt[a] for a in at], 1)
        if masked:
            q_pos = meta[2 * NK + i]
            u = lax.broadcasted_iota(jnp.int32, (BLK, 2 * BLK), 0)
            t = lax.broadcasted_iota(jnp.int32, (BLK, 2 * BLK), 1) % BLK
            ahead = t - u
            visible = [ahead >= (meta[NK + j * CHUNK + n] - q_pos) * BLK for n in range(CHUNK)]
        dv = jnp.zeros((keys, BLK), F32)
        dk = jnp.zeros((keys, BLK), F32)
        for pair in range(H // 2):
            cols = slice(pair * 2 * BLK, (pair + 1) * 2 * BLK)
            heads = [slice((2 * pair + g) * BLK, (2 * pair + g + 1) * BLK) for g in range(2)]
            score = jnp.dot(kb, qt[i, :, cols], preferred_element_type=F32)
            prob = jnp.exp2(score * factor - stats[pl.ds(i, 1), cols])
            if masked:
                prob = jnp.concatenate(
                    [
                        jnp.where(visible[n], prob[n * BLK : (n + 1) * BLK], 0.0)
                        for n in range(CHUNK)
                    ],
                    0,
                )
            d_prob = jnp.dot(vb, gt[i, :, cols], preferred_element_type=F32)
            d_score = (prob * (d_prob - stats[pl.ds(NQ + i, 1), cols])).astype(BF16)
            g_rows = jnp.concatenate([g_all[i, :, s] for s in heads], 0)
            q_rows = jnp.concatenate([q_all[i, :, s] for s in heads], 0)
            dv = dv + jnp.dot(prob.astype(BF16), g_rows, preferred_element_type=F32)
            dk = dk + jnp.dot(d_score, q_rows, preferred_element_type=F32)
            dqt[:, cols] += jnp.dot(ktb, d_score, preferred_element_type=F32)
        for n in range(CHUNK):
            dkv[at[n], :, :BLK] += dk[n * BLK : (n + 1) * BLK]
            dkv[at[n], :, BLK:] += dv[n * BLK : (n + 1) * BLK]

    def query_block(i, carry):
        dqt[...] = jnp.zeros_like(dqt)
        whole = meta[2 * NK + NQ + i]
        some = meta[2 * NK + 2 * NQ + i]

        def full_step(j, c):
            chunk(i, j, False)
            return c

        def masked_step(j, c):
            chunk(i, j, True)
            return c

        lax.fori_loop(0, whole, full_step, 0)
        lax.fori_loop(whole, some, masked_step, 0)
        rows = pl.ds(pl.multiple_of(i % 2 * BLK, BLK), BLK)

        def store(ref):
            for h in range(H):
                cols = slice(h * BLK, (h + 1) * BLK)
                ref[rows, cols] = (dqt[:, cols].T * scale).astype(ref.dtype)

        @pl.when(i < 2)
        def _():
            store(dq_own)

        @pl.when(i >= 2)
        def _():
            store(dq_other)

        return carry

    lax.fori_loop(0, NQ, query_block, 0)
    for b in range(8):
        for i in range(2):
            rows = slice(i * BLK, (i + 1) * BLK)
            ref = dkv_out[b]
            ref[rows, :BLK] = (dkv[2 * b + i, :, :BLK] * scale).astype(ref.dtype)
            ref[rows, BLK:] = dkv[2 * b + i, :, BLK:].astype(ref.dtype)


def attention(meta, queries, grads, stats, blocks):
    wide = H * BLK
    return pl.pallas_call(
        attn_kernel,
        out_shape=(
            jax.ShapeDtypeStruct((256, wide), F32),
            jax.ShapeDtypeStruct((256, wide), BF16),
            jax.ShapeDtypeStruct((256, 256), F32),
        )
        + (jax.ShapeDtypeStruct((256, 256), BF16),) * 7,
        in_specs=[smem()] + [vmem()] * 14,
        out_specs=(vmem(),) * 10,
        scratch_shapes=[
            pltpu.VMEM((NQ, BLK, wide), BF16),
            pltpu.VMEM((NQ, BLK, wide), BF16),
            pltpu.VMEM((NQ, BLK, wide), BF16),
            pltpu.VMEM((NQ, BLK, wide), BF16),
            pltpu.VMEM((NK, BLK, 2 * BLK), BF16),
            pltpu.VMEM((NK, BLK, BLK), BF16),
            pltpu.VMEM((BLK, wide), F32),
            pltpu.VMEM((NK, BLK, 2 * BLK), F32),
            pltpu.VMEM((2 * NQ, wide), F32),
        ],
        compiler_params=pltpu.CompilerParams(vmem_limit_bytes=VMEM_LIMIT),
        cost_estimate=pl.CostEstimate(
            flops=12 * 10**9, bytes_accessed=8 * 2**20, transcendentals=4 * 10**6
        ),
        name="attention",
    )(meta, *queries, *grads, *stats, *blocks)


def make_meta(k_pos, q_pos):
    order = jnp.argsort(k_pos).astype(jnp.int32)
    below = jnp.sum(k_pos[None, :] < q_pos[:, None], axis=1)
    reached = jnp.sum(k_pos[None, :] <= q_pos[:, None], axis=1)
    return jnp.concatenate(
        [order, k_pos[order], q_pos, below // CHUNK, (reached + CHUNK - 1) // CHUNK]
    ).astype(jnp.int32)


def project_kernel(place, mine_ref, other_ref, g_own, g_other, *refs):
    by_x_out, by_y_out = refs[0:4], refs[4:8]
    terms = refs[8]
    x, y = place[0], place[1]

    def step(z, carry):
        rows = pl.ds(pl.multiple_of(z * 512, 512), 512)
        terms[...] = jnp.dot(
            mine_ref[rows, :], g_own[...], preferred_element_type=F32
        ) + jnp.dot(other_ref[rows, :], g_other[...], preferred_element_type=F32)
        for k in range(4):
            x_to = (x + k) % 4
            for yl in range(YL):
                part = terms[pl.ds(pl.multiple_of(yl * 256 + x_to * 64, 64), 64), :BLK]
                at = pl.ds(pl.multiple_of(z * 128 + yl * 64, 64), 64)
                by_x_out[k][at, :] = part.astype(by_x_out[k].dtype)
            y_to = (y + k) % 4
            for xx in range(X):
                source = pl.multiple_of((y_to % 2) * 256 + xx * 64 + (y_to // 2) * 32, 32)
                part = terms[pl.ds(source, 32), BLK:]
                at = pl.ds(pl.multiple_of(z * 128 + xx * 32, 32), 32)
                by_y_out[k][at, :] = part.astype(by_y_out[k].dtype)
        return carry

    lax.fori_loop(0, Z, step, 0)


def project(place, mine, other, g_own, g_other):
    kept = jax.ShapeDtypeStruct((1024, BLK), F32)
    sent = jax.ShapeDtypeStruct((1024, BLK), BF16)
    return pl.pallas_call(
        project_kernel,
        out_shape=(kept, sent, sent, sent) * 2,
        in_specs=[smem()] + [vmem()] * 4,
        out_specs=(vmem(),) * 8,
        scratch_shapes=[pltpu.VMEM((512, 256), F32)],
        compiler_params=pltpu.CompilerParams(vmem_limit_bytes=VMEM_LIMIT),
        cost_estimate=pl.CostEstimate(
            flops=2 * 4096 * 512 * 256, bytes_accessed=8 * 2**20, transcendentals=0
        ),
        name="project",
    )(place, mine, other, g_own, g_other)


def second_kernel(place, *refs):
    a_in, b_in, a_out, b_out = refs[0:4], refs[4:8], refs[8:12], refs[12:16]
    a_sum, b_sum = refs[16:18]
    x, y = place[0], place[1]

    def total(parts):
        value = parts[0][...]
        for part in parts[1:]:
            value = value + part[...].astype(F32)
        return value

    a_sum[...] = total(a_in)
    b_sum[...] = total(b_in)
    for k in range(4):
        y_to = (y + k) % 4
        x_to = (x + k) % 4
        for z in range(Z):
            at = slice(z * 32, (z + 1) * 32)
            source = pl.multiple_of(z * 128 + (y_to % 2) * 64 + (y_to // 2) * 32, 32)
            a_out[k][at, :] = a_sum[pl.ds(source, 32), :].astype(a_out[k].dtype)
            source = pl.multiple_of(z * 128 + x_to * 32, 32)
            b_out[k][at, :] = b_sum[pl.ds(source, 32), :].astype(b_out[k].dtype)


def second(place, a_parts, b_parts):
    kept = jax.ShapeDtypeStruct((256, BLK), F32)
    sent = jax.ShapeDtypeStruct((256, BLK), BF16)
    return pl.pallas_call(
        second_kernel,
        out_shape=(kept, sent, sent, sent) * 2,
        in_specs=[smem()] + [vmem()] * 8,
        out_specs=(vmem(),) * 8,
        scratch_shapes=[pltpu.VMEM((1024, BLK), F32)] * 2,
        compiler_params=pltpu.CompilerParams(vmem_limit_bytes=VMEM_LIMIT),
        name="second",
    )(place, *a_parts, *b_parts)


def body(layer_input, query_rows, key_rows, value_rows, attn_out, d_attn, log_sum_exp, block_order):
    dp = lax.axis_index("dp")
    ctx = lax.axis_index("ctx")
    z, yl = dp // 2, dp % 2
    x, yh, c = ctx // 4, ctx // 2 % 2, ctx % 2
    y = 2 * yh + yl
    place = jnp.stack([x, y]).astype(jnp.int32)

    pair = jnp.concatenate([key_rows[0], value_rows[0]], axis=1)
    blocks = [pair] + [fetch(pair, by_ctx(*o)) for o in OFFSETS[1:]]
    q, g = query_rows[0], d_attn[0]
    q_other, g_other = fetch(q, swap_core), fetch(g, swap_core)
    mine, other, stats = prep(
        c.astype(jnp.int32)[None], layer_input[0], attn_out[0], g, log_sum_exp[0]
    )
    stats_other = fetch(stats, swap_core)
    mine_other = fetch(other, swap_core)

    owners = jnp.stack([(x + dx) % X * 4 + (yh ^ dyh) * 2 + c for dx, dyh in OFFSETS])
    slots = jnp.stack([2 * owners, 2 * owners + 1], axis=1).reshape(-1)
    q_slots = jnp.stack([2 * ctx, 2 * ctx + 1, 2 * (ctx ^ 1), 2 * (ctx ^ 1) + 1])
    meta = make_meta(block_order[slots], block_order[q_slots])
    dq_own, dq_sent, *dkv = attention(
        meta, (q, q_other), (g, g_other), (stats, stats_other), blocks
    )
    d_query = (dq_own + fetch(dq_sent, swap_core).astype(F32)).astype(BF16)[None]

    total = dkv[0]
    for (dx, dyh), part in zip(OFFSETS[1:], dkv[1:]):
        total = total + fetch(part, by_ctx(-dx, dyh)).astype(F32)
    grads = total.astype(BF16)
    grads_other = fetch(grads, swap_core)

    parts = project(place, mine, mine_other, grads, grads_other)
    a = [parts[0]] + [fetch(parts[k], by_x(-k)) for k in (1, 2, 3)]
    b = [parts[4]] + [fetch(parts[4 + k], by_y(-k)) for k in (1, 2, 3)]
    parts = second(place, a, b)
    a_sum, b_sum = parts[0], parts[4]
    for k in (1, 2, 3):
        a_sum = a_sum + fetch(parts[k], by_y(-k)).astype(F32)
        b_sum = b_sum + fetch(parts[4 + k], by_x(-k)).astype(F32)
    rest = jnp.concatenate([a_sum, b_sum], axis=1).reshape(4, 2, 32, 256)
    for bit in (1, 2, 4):
        own = (z // bit) % 2
        keep = lax.dynamic_index_in_dim(rest, own, 1, False)
        send = lax.dynamic_index_in_dim(rest, 1 - own, 1, False)
        rest = keep + fetch(send, by_z(bit))
        if bit < 4:
            rest = rest.reshape(rest.shape[0] // 2, 2, 32, 256)
    return (d_query, rest.reshape(32, 256))


def solution(mesh):
    return jax.shard_map(
        body,
        mesh=mesh,
        in_specs=(
            P("dp", "ctx", None),
            P("dp", "ctx", None),
            P("dp", "ctx", None),
            P("dp", "ctx", None),
            P("dp", "ctx", None),
            P("dp", "ctx", None),
            P("dp", None, "ctx"),
            P(),
        ),
        out_specs=(P("dp", "ctx", None), P(("dp", "ctx"), None)),
        check_vma=False,
    )
```

```python
import math

import jax
import jax.numpy as jnp
from jax import lax
from jax.experimental import pallas as pl
from jax.experimental.pallas import tpu as pltpu
from jax.sharding import PartitionSpec as P

F32 = jnp.float32
BF16 = jnp.bfloat16
BLK = 128
H = 8
Z, YL, X, YH, C = 8, 2, 4, 2, 2
AXES = ("z", "yl", "x", "yh", "c")
VMEM_LIMIT = 24 * 1024 * 1024


def coords(i):
    return (i // 32, i // 16 % 2, i // 4 % 4, i // 2 % 2, i % 2)


def index_of(z, yl, x, yh, c):
    return (((z * YL + yl) * X + x) * YH + yh) * C + c


def fetch(value, shift):
    pairs = [(index_of(*shift(*coords(i))), i) for i in range(Z * YL * X * YH * C)]
    return lax.ppermute(value, AXES, pairs)


def swap_core(z, yl, x, yh, c):
    return (z, yl, x, yh, 1 - c)


def by_ctx(dx, dyh):
    return lambda z, yl, x, yh, c: (z, yl, (x + dx) % X, yh ^ dyh, c)


def by_z(k):
    return lambda z, yl, x, yh, c: ((z + k) % Z, yl, x, yh, c)


FIRST = [(0, 0), (1, 0), (3, 0), (2, 0)]
SECOND = [(0, 1), (1, 1), (3, 1), (2, 1)]


def vmem():
    return pl.BlockSpec(memory_space=pltpu.VMEM)


def smem():
    return pl.BlockSpec(memory_space=pltpu.SMEM)


def anywhere():
    return pl.BlockSpec(memory_space=pl.ANY)


def stats_kernel(out_ref, grad_ref, lse_ref, stats_ref):
    for h in range(H):
        cols = slice(h * BLK, (h + 1) * BLK)
        product = out_ref[:, cols].astype(F32) * grad_ref[:, cols].astype(F32)
        delta = jnp.sum(product.T, axis=0, keepdims=True)
        lse2 = lse_ref[h : h + 1, :] * math.log2(math.e)
        for i in range(2):
            rows = slice(i * BLK, (i + 1) * BLK)
            stats_ref[i : i + 1, cols] = lse2[:, rows]
            stats_ref[2 + i : 3 + i, cols] = delta[:, rows]
    stats_ref[4:8, :] = jnp.zeros((4, H * BLK), F32)


def row_stats(saved, grad, lse):
    return pl.pallas_call(
        stats_kernel,
        out_shape=jax.ShapeDtypeStruct((8, H * BLK), F32),
        in_specs=[vmem()] * 3,
        out_specs=vmem(),
        compiler_params=pltpu.CompilerParams(vmem_limit_bytes=8 * 2**20),
        cost_estimate=pl.CostEstimate(flops=10**6, bytes_accessed=2**20, transcendentals=0),
        name="row_stats",
    )(saved, grad, lse)


def turn_kernel(me, x_ref, mine_ref, other_ref):
    even = me[0] == 0
    for u in range(8):
        tile = x_ref[:, u * BLK : (u + 1) * BLK].T
        for yh in range(YH):
            first = tile[yh * 64 : yh * 64 + 32]
            second = tile[yh * 64 + 32 : yh * 64 + 64]
            at = slice(u * 64 + yh * 32, u * 64 + yh * 32 + 32)

            @pl.when(even)
            def _():
                mine_ref[at, :] = first
                other_ref[at, :] = second

            @pl.when(jnp.logical_not(even))
            def _():
                mine_ref[at, :] = second
                other_ref[at, :] = first


def turn(me, layer):
    return pl.pallas_call(
        turn_kernel,
        grid=(Z,),
        out_shape=(jax.ShapeDtypeStruct((4096, 256), BF16),) * 2,
        in_specs=[smem(), pl.BlockSpec((256, 1024), lambda z: (0, z))],
        out_specs=(pl.BlockSpec((512, 256), lambda z: (z, 0)),) * 2,
        compiler_params=pltpu.CompilerParams(vmem_limit_bytes=8 * 2**20),
        cost_estimate=pl.CostEstimate(flops=10**7, bytes_accessed=8 * 2**20, transcendentals=0),
        name="turn",
    )(me, layer)


NQ, NK = 4, 8
SCALE = BLK**-0.5


def key_steps(meta, q_all, g_all, qt, gt, stats, kv, kt, dqt, dkv):
    factor = SCALE * math.log2(math.e)
    dkv[...] = jnp.zeros_like(dkv)

    def chunk(i, first, count, masked):
        keys = count * BLK
        at = [meta[first + n] for n in range(count)]
        rows = [pl.ds(pl.multiple_of(a * BLK, BLK), BLK) for a in at]
        kb = jnp.concatenate([kv[r, :BLK] for r in rows], 0)
        vb = jnp.concatenate([kv[r, BLK:] for r in rows], 0)
        ktb = jnp.concatenate([kt[a] for a in at], 1)
        if masked:
            q_pos = meta[2 * NK + i]
            u = lax.broadcasted_iota(jnp.int32, (BLK, 2 * BLK), 0)
            t = lax.broadcasted_iota(jnp.int32, (BLK, 2 * BLK), 1) % BLK
            ahead = t - u
            visible = [ahead >= (meta[NK + first + n] - q_pos) * BLK for n in range(count)]
        dv = jnp.zeros((keys, BLK), F32)
        dk = jnp.zeros((keys, BLK), F32)
        for pair in range(H // 2):
            cols = slice(pair * 2 * BLK, (pair + 1) * 2 * BLK)
            heads = [slice((2 * pair + g) * BLK, (2 * pair + g + 1) * BLK) for g in range(2)]
            score = jnp.dot(kb, qt[i, :, cols], preferred_element_type=F32)
            prob = jnp.exp2(score * factor - stats[pl.ds(i, 1), cols])
            if masked:
                prob = jnp.concatenate(
                    [
                        jnp.where(visible[n], prob[n * BLK : (n + 1) * BLK], 0.0)
                        for n in range(count)
                    ],
                    0,
                )
            d_prob = jnp.dot(vb, gt[i, :, cols], preferred_element_type=F32)
            d_score = (prob * (d_prob - stats[pl.ds(NQ + i, 1), cols])).astype(BF16)
            g_rows = jnp.concatenate([g_all[i, :, s] for s in heads], 0)
            q_rows = jnp.concatenate([q_all[i, :, s] for s in heads], 0)
            dv = dv + jnp.dot(prob.astype(BF16), g_rows, preferred_element_type=F32)
            dk = dk + jnp.dot(d_score, q_rows, preferred_element_type=F32)
            dqt[i, :, cols] += jnp.dot(ktb, d_score, preferred_element_type=F32)
        for n in range(count):
            dkv[at[n], :, :BLK] += dk[n * BLK : (n + 1) * BLK]
            dkv[at[n], :, BLK:] += dv[n * BLK : (n + 1) * BLK]

    def query_block(i, carry):
        whole = meta[2 * NK + NQ + i]
        pairs = meta[2 * NK + 2 * NQ + i]

        def full_step(j, c):
            chunk(i, 4 * j, 4, False)
            return c

        def pair_step(j, c):
            chunk(i, 4 * whole + 2 * j, 2, True)
            return c

        lax.fori_loop(0, whole, full_step, 0)
        lax.fori_loop(0, pairs, pair_step, 0)
        return carry

    lax.fori_loop(0, NQ, query_block, 0)


def store_keys(dkv, dkv_out):
    for b in range(4):
        for i in range(2):
            rows = slice(i * BLK, (i + 1) * BLK)
            ref = dkv_out[b]
            ref[rows, :BLK] = (dkv[2 * b + i, :, :BLK] * SCALE).astype(ref.dtype)
            ref[rows, BLK:] = dkv[2 * b + i, :, BLK:].astype(ref.dtype)


def first_kernel(meta, *refs):
    q_in, g_in, s_in, kv_in = refs[0:2], refs[2:4], refs[4:6], refs[6:10]
    q_all, g_all, qt, gt, stats, dqt = refs[10:16]
    dkv_out = refs[16:20]
    kv, kt, dkv, pieces, sems = refs[20:]
    copies = []
    for side in range(2):
        for i in range(2):
            rows = pl.ds(i * BLK, BLK)
            copies.append((q_in[side].at[rows], q_all.at[2 * side + i]))
            copies.append((g_in[side].at[rows], g_all.at[2 * side + i]))
        copies.append((s_in[side], pieces.at[side]))
    for b in range(4):
        copies.append((kv_in[b], kv.at[pl.ds(b * 2 * BLK, 2 * BLK)]))
    copies = [pltpu.make_async_copy(s, d, sems.at[n]) for n, (s, d) in enumerate(copies)]
    for copy in copies:
        copy.start()
    dqt[...] = jnp.zeros_like(dqt)
    for copy in copies:
        copy.wait()
    for side in range(2):
        stats[2 * side : 2 * side + 2, :] = pieces[side, 0:2, :]
        stats[NQ + 2 * side : NQ + 2 * side + 2, :] = pieces[side, 2:4, :]

    def transpose(n, carry):
        for h in range(H):
            cols = slice(h * BLK, (h + 1) * BLK)
            qt[n, :, cols] = q_all[n, :, cols].T
            gt[n, :, cols] = g_all[n, :, cols].T
        return carry

    lax.fori_loop(0, NQ, transpose, 0)
    for n in range(NK):
        kt[n] = kv[n * BLK : (n + 1) * BLK, :BLK].T
    key_steps(meta, q_all, g_all, qt, gt, stats, kv, kt, dqt, dkv)
    store_keys(dkv, dkv_out)


def second_kernel(meta, *refs):
    q_all, g_all, qt, gt, stats, dqt_in = refs[0:6]
    kv_in = refs[6:10]
    dq_own, dq_other = refs[10:12]
    dkv_out = refs[12:16]
    kv, kt, dkv, dqt, sems = refs[16:]
    copies = [
        pltpu.make_async_copy(kv_in[b], kv.at[pl.ds(b * 2 * BLK, 2 * BLK)], sems.at[b])
        for b in range(4)
    ]
    for copy in copies:
        copy.start()
    dqt[...] = dqt_in[...]
    for copy in copies:
        copy.wait()
    for n in range(NK):
        kt[n] = kv[n * BLK : (n + 1) * BLK, :BLK].T
    key_steps(meta, q_all, g_all, qt, gt, stats, kv, kt, dqt, dkv)
    store_keys(dkv, dkv_out)
    for n in range(NQ):
        ref = (dq_own, dq_own, dq_other, dq_other)[n]
        rows = slice(n % 2 * BLK, (n % 2 + 1) * BLK)
        for h in range(H):
            cols = slice(h * BLK, (h + 1) * BLK)
            ref[rows, cols] = (dqt[n, :, cols].T * SCALE).astype(ref.dtype)


WIDE = H * BLK
KEY_SCRATCH = [
    pltpu.VMEM((NK * BLK, 2 * BLK), BF16),
    pltpu.VMEM((NK, BLK, BLK), BF16),
    pltpu.VMEM((NK, BLK, 2 * BLK), F32),
]
COST = pl.CostEstimate(flops=6 * 10**10, bytes_accessed=2**20, transcendentals=2 * 10**6)


def dkv_shapes(own):
    return (jax.ShapeDtypeStruct((256, 256), own),) + (
        jax.ShapeDtypeStruct((256, 256), BF16),
    ) * 3


def first_call(meta, queries, grads, stats, blocks):
    rows = jax.ShapeDtypeStruct((NQ, BLK, WIDE), BF16)
    return pl.pallas_call(
        first_kernel,
        out_shape=(rows,) * 4
        + (
            jax.ShapeDtypeStruct((2 * NQ, WIDE), F32),
            jax.ShapeDtypeStruct((NQ, BLK, WIDE), F32),
        )
        + dkv_shapes(F32),
        in_specs=[smem()] + [anywhere()] * 10,
        out_specs=(vmem(),) * 10,
        scratch_shapes=KEY_SCRATCH
        + [pltpu.VMEM((2, 8, WIDE), F32), pltpu.SemaphoreType.DMA((14,))],
        compiler_params=pltpu.CompilerParams(vmem_limit_bytes=VMEM_LIMIT),
        cost_estimate=COST,
        name="attention_first",
    )(meta, *queries, *grads, *stats, *blocks)


def second_call(meta, carried, blocks):
    return pl.pallas_call(
        second_kernel,
        out_shape=(
            jax.ShapeDtypeStruct((256, WIDE), F32),
            jax.ShapeDtypeStruct((256, WIDE), BF16),
        )
        + dkv_shapes(BF16),
        in_specs=[smem()] + [vmem()] * 6 + [anywhere()] * 4,
        out_specs=(vmem(),) * 6,
        scratch_shapes=KEY_SCRATCH
        + [pltpu.VMEM((NQ, BLK, WIDE), F32), pltpu.SemaphoreType.DMA((4,))],
        compiler_params=pltpu.CompilerParams(vmem_limit_bytes=VMEM_LIMIT),
        cost_estimate=COST,
        name="attention_second",
    )(meta, *carried, *blocks)


def make_meta(k_pos, q_pos):
    rank = jnp.sum(k_pos[None, :] < k_pos[:, None], axis=1)
    hit = rank[None, :] == jnp.arange(NK)[:, None]
    order = jnp.sum(jnp.where(hit, jnp.arange(NK)[None, :], 0), axis=1)
    ordered = jnp.sum(jnp.where(hit, k_pos[None, :], 0), axis=1)
    below = jnp.sum(k_pos[None, :] < q_pos[:, None], axis=1)
    reached = jnp.sum(k_pos[None, :] <= q_pos[:, None], axis=1)
    whole = below // 4
    pairs = (reached - 4 * whole + 1) // 2
    return jnp.concatenate([order, ordered, q_pos, whole, pairs]).astype(jnp.int32)


def project_kernel(mine_ref, other_ref, g_own, g_other, out_ref):
    def step(z, carry):
        rows = pl.ds(pl.multiple_of(z * 512, 512), 512)
        terms = jnp.dot(mine_ref[rows, :], g_own[...], preferred_element_type=F32) + jnp.dot(
            other_ref[rows, :], g_other[...], preferred_element_type=F32
        )
        at = pl.ds(pl.multiple_of(z * 32, 32), 32)
        out_ref[:, at, :] = terms.astype(BF16).reshape(16, 32, 256)
        return carry

    lax.fori_loop(0, Z, step, 0)


def project(mine, other, g_own, g_other):
    return pl.pallas_call(
        project_kernel,
        out_shape=jax.ShapeDtypeStruct((16, 256, 256), BF16),
        in_specs=[vmem()] * 4,
        out_specs=vmem(),
        compiler_params=pltpu.CompilerParams(vmem_limit_bytes=16 * 2**20),
        cost_estimate=pl.CostEstimate(
            flops=2 * 4096 * 512 * 256, bytes_accessed=8 * 2**20, transcendentals=0
        ),
        name="project",
    )(mine, other, g_own, g_other)


def sum_kernel(place, in_ref, own_ref, *out_refs):
    for k in range(Z):
        at = pl.ds(pl.multiple_of((place[0] + k) % Z * 32, 32), 32)
        value = in_ref[0, at, :].astype(F32)
        for j in range(1, 16):
            value = value + in_ref[j, at, :].astype(F32)
        ref = own_ref if k == 0 else out_refs[k - 1]
        ref[...] = value.astype(ref.dtype)


def sum_terms(place, terms):
    return pl.pallas_call(
        sum_kernel,
        out_shape=(jax.ShapeDtypeStruct((32, 256), F32),)
        + (jax.ShapeDtypeStruct((32, 256), BF16),) * 7,
        in_specs=[smem(), vmem()],
        out_specs=(vmem(),) * 8,
        compiler_params=pltpu.CompilerParams(vmem_limit_bytes=8 * 2**20),
        name="sum_terms",
    )(place, terms)


def body(layer_input, query_rows, key_rows, value_rows, attn_out, d_attn, log_sum_exp, block_order):
    z, x, yh, c = (lax.axis_index(name) for name in ("z", "x", "yh", "c"))
    ctx = (x * YH + yh) * C + c

    q, g = query_rows[0], d_attn[0]
    pair = jnp.concatenate([key_rows[0], value_rows[0]], axis=1)
    blocks = [pair] + [fetch(pair, by_ctx(*o)) for o in FIRST[1:]]
    q_other, g_other = fetch(q, swap_core), fetch(g, swap_core)
    stats = row_stats(attn_out[0], g, log_sum_exp[0])
    stats_other = fetch(stats, swap_core)
    mine, other = turn(c.astype(jnp.int32)[None], layer_input[0])

    places = block_order.reshape(16, 2)
    q_pos = jnp.concatenate([places[ctx], places[ctx ^ 1]])

    def owners(group):
        return jnp.concatenate(
            [places[(x + dx) % X * 4 + (yh ^ dyh) * 2 + c] for dx, dyh in group]
        )

    pair_again, *blocks = lax.optimization_barrier((pair, *blocks))
    later = [fetch(pair_again, by_ctx(*o)) for o in SECOND]
    blocks, mine, other = lax.optimization_barrier((blocks, mine, other))
    outs = first_call(
        make_meta(owners(FIRST), q_pos), (q, q_other), (g, g_other), (stats, stats_other), blocks
    )
    outs, other = lax.optimization_barrier((outs, other))
    carried, dkv_first = outs[:6], outs[6:]
    mine_other = fetch(other, swap_core)
    dq_own, dq_sent, *dkv_second = second_call(make_meta(owners(SECOND), q_pos), carried, later)
    total = dkv_first[0]
    for (dx, dyh), part in zip(FIRST[1:], dkv_first[1:]):
        total = total + fetch(part, by_ctx(-dx, dyh)).astype(F32)
    total, dkv_second = lax.optimization_barrier((total, dkv_second))
    for (dx, dyh), part in zip(SECOND, dkv_second):
        total = total + fetch(part, by_ctx(-dx, dyh)).astype(F32)
    grads = total.astype(BF16)
    grads_other = fetch(grads, swap_core)
    d_query = (dq_own + fetch(dq_sent, swap_core).astype(F32)).astype(BF16)[None]

    terms = project(mine, mine_other, grads, grads_other)
    terms = lax.all_to_all(terms, ("yl", "x", "yh"), 0, 0)
    own, *sent = sum_terms(z.astype(jnp.int32)[None], terms)
    for k in range(1, Z):
        own = own + fetch(sent[k - 1], by_z(-k)).astype(F32)
    return (d_query, own)


def solution(mesh):
    fine = jax.sharding.Mesh(mesh.devices.reshape(Z, YL, X, YH, C), AXES)
    dp, ctx = ("z", "yl"), ("x", "yh", "c")
    rows = P(dp, ctx, None)
    return jax.shard_map(
        body,
        mesh=fine,
        in_specs=(rows, rows, rows, rows, rows, rows, P(dp, None, ctx), P()),
        out_specs=(rows, P(AXES, None)),
        check_vma=False,
    )
```

```python
import functools
import math

import jax
import jax.numpy as jnp
from jax import lax
from jax.experimental import pallas as pl
from jax.experimental.pallas import tpu as pltpu
from jax.sharding import PartitionSpec as P

F32 = jnp.float32
BF16 = jnp.bfloat16
BLK = 128
H = 8
Z, YL, X, YH, C = 8, 2, 4, 2, 2
AXES = ("z", "yl", "x", "yh", "c")
VMEM_LIMIT = 24 * 1024 * 1024


def coords(i):
    return (i // 32, i // 16 % 2, i // 4 % 4, i // 2 % 2, i % 2)


def index_of(z, yl, x, yh, c):
    return (((z * YL + yl) * X + x) * YH + yh) * C + c


def fetch(value, shift):
    pairs = [(index_of(*shift(*coords(i))), i) for i in range(Z * YL * X * YH * C)]
    return lax.ppermute(value, AXES, pairs)


def swap_core(z, yl, x, yh, c):
    return (z, yl, x, yh, 1 - c)


def by_ctx(dx, dyh):
    return lambda z, yl, x, yh, c: (z, yl, (x + dx) % X, yh ^ dyh, c)


def by_z(k):
    return lambda z, yl, x, yh, c: ((z + k) % Z, yl, x, yh, c)


def swap_z(z, yl, x, yh, c):
    return (z ^ 1, yl, x, yh, c)


ALONG_X = (0, 1, 3, 2)


def vmem():
    return pl.BlockSpec(memory_space=pltpu.VMEM)


def smem():
    return pl.BlockSpec(memory_space=pltpu.SMEM)


def anywhere():
    return pl.BlockSpec(memory_space=pl.ANY)


def hbm():
    return pl.BlockSpec(memory_space=pltpu.HBM)


def stats_kernel(out_hbm, grad_hbm, lse_hbm, stats_ref, out_ref, grad_ref, lse_ref, sems):
    pairs = ((out_hbm, out_ref), (grad_hbm, grad_ref), (lse_hbm, lse_ref))
    copies = [pltpu.make_async_copy(a, b, sems.at[n]) for n, (a, b) in enumerate(pairs)]
    for copy in copies:
        copy.start()
    stats_ref[4:8, :] = jnp.zeros((4, H * BLK), F32)
    for copy in copies:
        copy.wait()
    for h in range(H):
        cols = slice(h * BLK, (h + 1) * BLK)
        product = out_ref[:, cols].astype(F32) * grad_ref[:, cols].astype(F32)
        delta = jnp.sum(product.T, axis=0, keepdims=True)
        lse2 = lse_ref[h : h + 1, :] * math.log2(math.e)
        for i in range(2):
            rows = slice(i * BLK, (i + 1) * BLK)
            stats_ref[i : i + 1, cols] = lse2[:, rows]
            stats_ref[2 + i : 3 + i, cols] = delta[:, rows]


def row_stats(saved, grad, lse):
    return pl.pallas_call(
        stats_kernel,
        out_shape=jax.ShapeDtypeStruct((8, H * BLK), F32),
        in_specs=[hbm()] * 3,
        out_specs=vmem(),
        scratch_shapes=[
            pltpu.VMEM((256, H * BLK), BF16),
            pltpu.VMEM((256, H * BLK), BF16),
            pltpu.VMEM((H, 256), F32),
            pltpu.SemaphoreType.DMA((3,)),
        ],
        compiler_params=pltpu.CompilerParams(vmem_limit_bytes=8 * 2**20),
        cost_estimate=pl.CostEstimate(flops=10**6, bytes_accessed=2**20, transcendentals=0),
        name="row_stats",
    )(saved, grad, lse)


SLABS = Z // 2


def cut_kernel(place, x_ref, k_ref, v_ref, a_ref, b_ref, own_ref, pair_ref, sems):
    moves = [
        (k_ref, pair_ref.at[:, pl.ds(0, BLK)]),
        (v_ref, pair_ref.at[:, pl.ds(BLK, BLK)]),
    ]
    for j in range(SLABS):
        at = pl.ds(pl.multiple_of((2 * j + 1 - place[1]) * 1024, 1024), 1024)
        moves.append((x_ref.at[:, at], (a_ref, b_ref)[j // 2].at[j % 2]))
    for j in range(SLABS):
        at = pl.ds(pl.multiple_of((2 * j + place[1]) * 1024, 1024), 1024)
        moves.append((x_ref.at[:, at], own_ref.at[j]))
    copies = [pltpu.make_async_copy(a, b, sems.at[n]) for n, (a, b) in enumerate(moves)]
    for copy in copies:
        copy.start()
    for copy in copies:
        copy.wait()


def cut(place, layer, keys, values):
    half = jax.ShapeDtypeStruct((SLABS // 2, 256, 1024), BF16)
    return pl.pallas_call(
        cut_kernel,
        out_shape=(
            half,
            half,
            jax.ShapeDtypeStruct((SLABS, 256, 1024), BF16),
            jax.ShapeDtypeStruct((256, 2 * BLK), BF16),
        ),
        in_specs=[smem()] + [hbm()] * 3,
        out_specs=(anywhere(),) * 4,
        scratch_shapes=[pltpu.SemaphoreType.DMA((2 + 2 * SLABS,))],
        compiler_params=pltpu.CompilerParams(vmem_limit_bytes=57 * 2**20),
        name="cut",
    )(place, layer, keys, values)


def turn_kernel(place, *refs):
    x_refs = refs[:-4]
    mine_ref, other_ref, slabs, sems = refs[-4:]
    copies = []
    for j in range(SLABS):
        each = SLABS // len(x_refs)
        source = x_refs[j // each].at[j % each]
        copies.append(pltpu.make_async_copy(source, slabs.at[j], sems.at[j]))
    for copy in copies:
        copy.start()
    even = place[0] == 0
    for j in range(SLABS):
        copies[j].wait()
        for u in range(8):
            tile = slabs[j, :, u * BLK : (u + 1) * BLK].T
            for yh in range(YH):
                first = tile[yh * 64 : yh * 64 + 32]
                second = tile[yh * 64 + 32 : yh * 64 + 64]
                start = j * 512 + u * 64 + yh * 32
                at = slice(start, start + 32)

                @pl.when(even)
                def _():
                    mine_ref[at, :] = first
                    other_ref[at, :] = second

                @pl.when(jnp.logical_not(even))
                def _():
                    mine_ref[at, :] = second
                    other_ref[at, :] = first


def turn(place, *layers):
    return pl.pallas_call(
        turn_kernel,
        out_shape=(jax.ShapeDtypeStruct((2048, 256), BF16),) * 2,
        in_specs=[smem()] + [anywhere()] * len(layers),
        out_specs=(vmem(),) * 2,
        scratch_shapes=[
            pltpu.VMEM((SLABS, 256, 1024), BF16),
            pltpu.SemaphoreType.DMA((SLABS,)),
        ],
        compiler_params=pltpu.CompilerParams(vmem_limit_bytes=8 * 2**20),
        cost_estimate=pl.CostEstimate(flops=3 * 10**10, bytes_accessed=8 * 2**20, transcendentals=0),
        name="turn",
    )(place, *layers)


NQ, NK = 4, 8
SCALE = BLK**-0.5


def key_steps(meta, q_all, g_all, qt, gt, stats, kv, kt, dqt, dkv):
    factor = SCALE * math.log2(math.e)
    dkv[...] = jnp.zeros_like(dkv)

    def chunk(i, first, count, masked):
        keys = count * BLK
        at = [meta[first + n] for n in range(count)]
        rows = [pl.ds(pl.multiple_of(a * BLK, BLK), BLK) for a in at]
        kb = jnp.concatenate([kv[r, :BLK] for r in rows], 0)
        vb = jnp.concatenate([kv[r, BLK:] for r in rows], 0)
        ktb = jnp.concatenate([kt[a] for a in at], 1)
        if masked:
            q_pos = meta[2 * NK + i]
            u = lax.broadcasted_iota(jnp.int32, (BLK, 2 * BLK), 0)
            t = lax.broadcasted_iota(jnp.int32, (BLK, 2 * BLK), 1) % BLK
            ahead = t - u
            visible = [ahead >= (meta[NK + first + n] - q_pos) * BLK for n in range(count)]
        dv = jnp.zeros((keys, BLK), F32)
        dk = jnp.zeros((keys, BLK), F32)
        for pair in range(H // 2):
            cols = slice(pair * 2 * BLK, (pair + 1) * 2 * BLK)
            heads = [slice((2 * pair + g) * BLK, (2 * pair + g + 1) * BLK) for g in range(2)]
            score = jnp.dot(kb, qt[i, :, cols], preferred_element_type=F32)
            prob = jnp.exp2(score * factor - stats[pl.ds(i, 1), cols])
            if masked:
                prob = jnp.concatenate(
                    [
                        jnp.where(visible[n], prob[n * BLK : (n + 1) * BLK], 0.0)
                        for n in range(count)
                    ],
                    0,
                )
            d_prob = jnp.dot(vb, gt[i, :, cols], preferred_element_type=F32)
            d_score = (prob * (d_prob - stats[pl.ds(NQ + i, 1), cols])).astype(BF16)
            g_rows = jnp.concatenate([g_all[i, :, s] for s in heads], 0)
            q_rows = jnp.concatenate([q_all[i, :, s] for s in heads], 0)
            dv = dv + jnp.dot(prob.astype(BF16), g_rows, preferred_element_type=F32)
            dk = dk + jnp.dot(d_score, q_rows, preferred_element_type=F32)
            dqt[i, :, cols] += jnp.dot(ktb, d_score, preferred_element_type=F32)
        for n in range(count):
            dkv[at[n], :, :BLK] += dk[n * BLK : (n + 1) * BLK]
            dkv[at[n], :, BLK:] += dv[n * BLK : (n + 1) * BLK]

    def query_block(i, carry):
        whole = meta[2 * NK + NQ + i]
        pairs = meta[2 * NK + 2 * NQ + i]

        def full_step(j, c):
            chunk(i, 4 * j, 4, False)
            return c

        def pair_step(j, c):
            chunk(i, 4 * whole + 2 * j, 2, True)
            return c

        lax.fori_loop(0, whole, full_step, 0)
        lax.fori_loop(0, pairs, pair_step, 0)
        return carry

    lax.fori_loop(0, NQ, query_block, 0)


def store_keys(dkv, refs):
    for n in range(NK):
        b, i = n // 2, n % 2
        ref = refs[b]
        rows = slice(i * BLK, (i + 1) * BLK)
        ref[rows, :BLK] = (dkv[n, :, :BLK] * SCALE).astype(ref.dtype)
        ref[rows, BLK:] = dkv[n, :, BLK:].astype(ref.dtype)


def first_kernel(meta, *refs):
    q_in, g_in, s_in, kv_in = refs[0:2], refs[2:4], refs[4:6], refs[6:10]
    q_all, g_all, qt, gt, stats, dqt = refs[10:16]
    dkv_out = refs[16]
    kv, kt, dkv, pieces, sems = refs[17:]
    copies = []
    for side in range(2):
        for i in range(2):
            rows = pl.ds(i * BLK, BLK)
            copies.append((q_in[side].at[rows], q_all.at[2 * side + i]))
            copies.append((g_in[side].at[rows], g_all.at[2 * side + i]))
        copies.append((s_in[side], pieces.at[side]))
    for b in range(4):
        source = kv_in[b].at[pl.ds(2 * BLK, 2 * BLK)]
        copies.append((source, kv.at[pl.ds(b * 2 * BLK, 2 * BLK)]))
    copies = [pltpu.make_async_copy(s, d, sems.at[n]) for n, (s, d) in enumerate(copies)]
    for copy in copies:
        copy.start()
    dqt[...] = jnp.zeros_like(dqt)
    for copy in copies:
        copy.wait()
    for side in range(2):
        stats[2 * side : 2 * side + 2, :] = pieces[side, 0:2, :]
        stats[NQ + 2 * side : NQ + 2 * side + 2, :] = pieces[side, 2:4, :]

    def transpose(n, carry):
        for h in range(H):
            cols = slice(h * BLK, (h + 1) * BLK)
            qt[n, :, cols] = q_all[n, :, cols].T
            gt[n, :, cols] = g_all[n, :, cols].T
        return carry

    lax.fori_loop(0, NQ, transpose, 0)
    for n in range(NK):
        kt[n] = kv[n * BLK : (n + 1) * BLK, :BLK].T
    key_steps(meta, q_all, g_all, qt, gt, stats, kv, kt, dqt, dkv)
    store_keys(dkv, [dkv_out.at[pl.ds(b * 2 * BLK, 2 * BLK)] for b in range(4)])


def second_kernel(meta, *refs):
    q_all, g_all, qt, gt, stats, dqt_in = refs[0:6]
    kv_in = refs[6:10]
    dq_own, dq_other = refs[10:12]
    dkv_out = refs[12:16]
    kv, kt, dkv, dqt, sems = refs[16:]
    copies = [
        pltpu.make_async_copy(
            kv_in[b].at[pl.ds(0, 2 * BLK)], kv.at[pl.ds(b * 2 * BLK, 2 * BLK)], sems.at[b]
        )
        for b in range(4)
    ]
    for copy in copies:
        copy.start()
    dqt[...] = dqt_in[...]
    for copy in copies:
        copy.wait()
    for n in range(NK):
        kt[n] = kv[n * BLK : (n + 1) * BLK, :BLK].T
    key_steps(meta, q_all, g_all, qt, gt, stats, kv, kt, dqt, dkv)
    store_keys(dkv, dkv_out)
    for n in range(NQ):
        ref = (dq_own, dq_own, dq_other, dq_other)[n]
        rows = slice(n % 2 * BLK, (n % 2 + 1) * BLK)
        for h in range(H):
            cols = slice(h * BLK, (h + 1) * BLK)
            ref[rows, cols] = (dqt[n, :, cols].T * SCALE).astype(ref.dtype)


WIDE = H * BLK
KEY_SCRATCH = [
    pltpu.VMEM((NK * BLK, 2 * BLK), BF16),
    pltpu.VMEM((NK, BLK, BLK), BF16),
    pltpu.VMEM((NK, BLK, 2 * BLK), F32),
]
COST = pl.CostEstimate(flops=6 * 10**10, bytes_accessed=2**20, transcendentals=2 * 10**6)


def first_call(meta, queries, grads, stats, blocks):
    rows = jax.ShapeDtypeStruct((NQ, BLK, WIDE), BF16)
    return pl.pallas_call(
        first_kernel,
        out_shape=(rows,) * 4
        + (
            jax.ShapeDtypeStruct((2 * NQ, WIDE), F32),
            jax.ShapeDtypeStruct((NQ, BLK, WIDE), F32),
        )
        + (jax.ShapeDtypeStruct((NK * BLK, 2 * BLK), BF16),),
        in_specs=[smem()] + [hbm(), anywhere()] * 2 + [anywhere()] * 6,
        out_specs=(vmem(),) * 7,
        scratch_shapes=KEY_SCRATCH
        + [pltpu.VMEM((2, 8, WIDE), F32), pltpu.SemaphoreType.DMA((14,))],
        compiler_params=pltpu.CompilerParams(vmem_limit_bytes=VMEM_LIMIT),
        cost_estimate=COST,
        name="attention_first",
    )(meta, *queries, *grads, *stats, *blocks)


def second_call(meta, carried, blocks):
    return pl.pallas_call(
        second_kernel,
        out_shape=(
            jax.ShapeDtypeStruct((256, WIDE), F32),
            jax.ShapeDtypeStruct((256, WIDE), BF16),
        )
        + (jax.ShapeDtypeStruct((2 * BLK, 2 * BLK), F32),) * 4,
        in_specs=[smem()] + [vmem()] * 6 + [anywhere()] * 4,
        out_specs=(vmem(),) * 6,
        scratch_shapes=KEY_SCRATCH
        + [pltpu.VMEM((NQ, BLK, WIDE), F32), pltpu.SemaphoreType.DMA((4,))],
        compiler_params=pltpu.CompilerParams(vmem_limit_bytes=VMEM_LIMIT),
        cost_estimate=COST,
        name="attention_second",
    )(meta, *carried, *blocks)


def make_meta(k_pos, q_pos):
    rank = jnp.sum(k_pos[None, :] < k_pos[:, None], axis=1)
    hit = rank[None, :] == jnp.arange(NK)[:, None]
    order = jnp.sum(jnp.where(hit, jnp.arange(NK)[None, :], 0), axis=1)
    ordered = jnp.sum(jnp.where(hit, k_pos[None, :], 0), axis=1)
    below = jnp.sum(k_pos[None, :] < q_pos[:, None], axis=1)
    reached = jnp.sum(k_pos[None, :] <= q_pos[:, None], axis=1)
    whole = below // 4
    pairs = (reached - 4 * whole + 1) // 2
    return jnp.concatenate([order, ordered, q_pos, whole, pairs]).astype(jnp.int32)


def project_kernel(a_ref, b_ref, c_ref, d_ref, ga, gb, gc, gd, out_ref):
    sides = ((a_ref, ga), (b_ref, gb), (c_ref, gc), (d_ref, gd))

    def step(j, carry):
        rows = pl.ds(pl.multiple_of(j * 512, 512), 512)
        terms = jnp.zeros((512, 256), F32)
        for turned, grads in sides:
            terms = terms + jnp.dot(turned[rows, :], grads[...], preferred_element_type=F32)
        at = pl.ds(pl.multiple_of(j * 32, 32), 32)
        out_ref[:, at, :] = terms.astype(BF16).reshape(16, 32, 256)
        return carry

    lax.fori_loop(0, SLABS, step, 0)


def project(turned, grads):
    return pl.pallas_call(
        project_kernel,
        out_shape=jax.ShapeDtypeStruct((16, SLABS * 32, 256), BF16),
        in_specs=[vmem()] * 8,
        out_specs=vmem(),
        compiler_params=pltpu.CompilerParams(vmem_limit_bytes=12 * 2**20),
        cost_estimate=pl.CostEstimate(
            flops=2 * 4096 * 512 * 256, bytes_accessed=8 * 2**20, transcendentals=0
        ),
        name="project",
    )(*turned, *grads)


def sum_kernel(place, in_ref, own_ref, *out_refs):
    for k in range(SLABS):
        at = pl.ds(pl.multiple_of((place[2] + k) % SLABS * 32, 32), 32)
        value = in_ref[0, at, :].astype(F32)
        for j in range(1, 16):
            value = value + in_ref[j, at, :].astype(F32)
        ref = own_ref if k == 0 else out_refs[k - 1]
        ref[...] = value.astype(ref.dtype)


def sum_terms(place, terms):
    return pl.pallas_call(
        sum_kernel,
        out_shape=(jax.ShapeDtypeStruct((32, 256), F32),)
        + (jax.ShapeDtypeStruct((32, 256), BF16),) * (SLABS - 1),
        in_specs=[smem(), vmem()],
        out_specs=(vmem(),) * SLABS,
        compiler_params=pltpu.CompilerParams(vmem_limit_bytes=8 * 2**20),
        name="sum_terms",
    )(place, terms)


def body(layer_input, query_rows, key_rows, value_rows, attn_out, d_attn, log_sum_exp, block_order):
    z, x, yh, c = (lax.axis_index(name) for name in ("z", "x", "yh", "c"))
    ctx = (x * YH + yh) * C + c
    place = jnp.stack([c, z % 2, z // 2]).astype(jnp.int32)

    q, g = query_rows[0], d_attn[0]
    cut_a, cut_b, cut_own, pair = cut(place, layer_input[0], key_rows[0], value_rows[0])
    pair_y = fetch(pair, by_ctx(0, 1))
    q_other, g_other = fetch(q, swap_core), fetch(g, swap_core)
    slabs_a = fetch(cut_a, swap_z)
    stats = row_stats(attn_out[0], g, log_sum_exp[0])
    stats_other = fetch(stats, swap_core)
    both = jnp.concatenate([pair, pair_y], axis=0)
    blocks = [both] + [fetch(both, by_ctx(k, 0)) for k in ALONG_X[1:]]
    mine, other = turn(place, cut_own)

    places = block_order.reshape(16, 2)
    q_pos = jnp.concatenate([places[ctx], places[ctx ^ 1]])

    def owners(row):
        return jnp.concatenate([places[(x + k) % X * 4 + row * 2 + c] for k in ALONG_X])

    blocks, mine, other, slabs_a = lax.optimization_barrier((blocks, mine, other, slabs_a))
    slabs_b = fetch(cut_b, swap_z)
    mine_core = fetch(other, swap_core)
    *carried, dkv_y = first_call(
        make_meta(owners(1 - yh), q_pos), (q, q_other), (g, g_other), (stats, stats_other), blocks
    )
    carried, mine_core = lax.optimization_barrier((carried, mine_core))
    dq_own, dq_sent, *dkv = second_call(make_meta(owners(yh), q_pos), carried, blocks)
    dkv_y = fetch(dkv_y, by_ctx(0, 1))
    dkv = [part + dkv_y[256 * b : 256 * b + 256].astype(F32) for b, part in enumerate(dkv)]
    parts = [fetch(part.astype(BF16), by_ctx(-k, 0)) for k, part in zip(ALONG_X[1:], dkv[1:])]
    total = dkv[0]
    for part in parts:
        total = total + part.astype(F32)
    grads = total.astype(BF16)
    grads_z = fetch(grads, swap_z)
    grads_core = fetch(grads, swap_core)
    slabs_a, slabs_b, grads_core = lax.optimization_barrier((slabs_a, slabs_b, grads_core))
    grads_zc = fetch(grads_z, swap_core)
    mine_z, other_z = turn(place, slabs_a, slabs_b)
    mine_zc = fetch(other_z, swap_core)

    terms = project(
        (mine, mine_core, mine_z, mine_zc), (grads, grads_core, grads_z, grads_zc)
    )
    terms = lax.all_to_all(terms, ("yl", "x", "yh"), 0, 0)
    terms, dq_sent = lax.optimization_barrier((terms, dq_sent))
    own, *sent = sum_terms(place, terms)
    d_query = (dq_own + fetch(dq_sent, swap_core).astype(F32)).astype(BF16)[None]
    for k in range(1, SLABS):
        own = own + fetch(sent[k - 1], by_z(-2 * k)).astype(F32)
    return (d_query, own)


def solution(mesh):
    fine = jax.sharding.Mesh(mesh.devices.reshape(Z, YL, X, YH, C), AXES)
    dp, ctx = ("z", "yl"), ("x", "yh", "c")
    rows = P(dp, ctx, None)
    return jax.shard_map(
        body,
        mesh=fine,
        in_specs=(rows, rows, rows, rows, rows, rows, P(dp, None, ctx), P()),
        out_specs=(rows, P(AXES, None)),
        check_vma=False,
    )
```

```python
import math

import jax
import jax.numpy as jnp
from jax import lax
from jax.experimental import pallas as pl
from jax.experimental.pallas import tpu as pltpu
from jax.sharding import PartitionSpec as P

F32 = jnp.float32
BF16 = jnp.bfloat16
BLK = 128
H = 8
Z, YL, X, YH, C = 8, 2, 4, 2, 2
AXES = ("z", "yl", "x", "yh", "c")
VMEM_LIMIT = 24 * 1024 * 1024


def coords(i):
    return (i // 32, i // 16 % 2, i // 4 % 4, i // 2 % 2, i % 2)


def index_of(z, yl, x, yh, c):
    return (((z * YL + yl) * X + x) * YH + yh) * C + c


def fetch(value, shift):
    pairs = [(index_of(*shift(*coords(i))), i) for i in range(Z * YL * X * YH * C)]
    return lax.ppermute(value, AXES, pairs)


def swap_core(z, yl, x, yh, c):
    return (z, yl, x, yh, 1 - c)


def by_ctx(dx, dyh):
    return lambda z, yl, x, yh, c: (z, yl, (x + dx) % X, yh ^ dyh, c)


def by_z(k):
    return lambda z, yl, x, yh, c: ((z + k) % Z, yl, x, yh, c)


def swap_z(z, yl, x, yh, c):
    return (z ^ 1, yl, x, yh, c)


ALONG_X = (0, 1, 3, 2)


def vmem():
    return pl.BlockSpec(memory_space=pltpu.VMEM)


def smem():
    return pl.BlockSpec(memory_space=pltpu.SMEM)


def anywhere():
    return pl.BlockSpec(memory_space=pl.ANY)


def hbm():
    return pl.BlockSpec(memory_space=pltpu.HBM)


def stats_kernel(out_hbm, grad_hbm, lse_hbm, stats_ref, out_ref, grad_ref, lse_ref, sems):
    pairs = ((out_hbm, out_ref), (grad_hbm, grad_ref), (lse_hbm, lse_ref))
    copies = [pltpu.make_async_copy(a, b, sems.at[n]) for n, (a, b) in enumerate(pairs)]
    for copy in copies:
        copy.start()
    stats_ref[4:8, :] = jnp.zeros((4, H * BLK), F32)
    for copy in copies:
        copy.wait()
    for h in range(H):
        cols = slice(h * BLK, (h + 1) * BLK)
        product = out_ref[:, cols].astype(F32) * grad_ref[:, cols].astype(F32)
        delta = jnp.sum(product.T, axis=0, keepdims=True)
        lse2 = lse_ref[h : h + 1, :] * math.log2(math.e)
        for i in range(2):
            rows = slice(i * BLK, (i + 1) * BLK)
            stats_ref[i : i + 1, cols] = lse2[:, rows]
            stats_ref[2 + i : 3 + i, cols] = delta[:, rows]


def row_stats(saved, grad, lse):
    return pl.pallas_call(
        stats_kernel,
        out_shape=jax.ShapeDtypeStruct((8, H * BLK), F32),
        in_specs=[hbm()] * 3,
        out_specs=vmem(),
        scratch_shapes=[
            pltpu.VMEM((256, H * BLK), BF16),
            pltpu.VMEM((256, H * BLK), BF16),
            pltpu.VMEM((H, 256), F32),
            pltpu.SemaphoreType.DMA((3,)),
        ],
        compiler_params=pltpu.CompilerParams(vmem_limit_bytes=8 * 2**20),
        cost_estimate=pl.CostEstimate(flops=10**6, bytes_accessed=2**20, transcendentals=0),
        name="row_stats",
    )(saved, grad, lse)


def turn_kernel(me, x_ref, mine_ref, other_ref):
    even = me[0] == 0
    for u in range(8):
        tile = x_ref[:, u * BLK : (u + 1) * BLK].T
        for yh in range(YH):
            first = tile[yh * 64 : yh * 64 + 32]
            second = tile[yh * 64 + 32 : yh * 64 + 64]
            at = slice(u * 64 + yh * 32, u * 64 + yh * 32 + 32)

            @pl.when(even)
            def _():
                mine_ref[at, :] = first
                other_ref[at, :] = second

            @pl.when(jnp.logical_not(even))
            def _():
                mine_ref[at, :] = second
                other_ref[at, :] = first


def turn(me, layer):
    return pl.pallas_call(
        turn_kernel,
        grid=(Z,),
        out_shape=(jax.ShapeDtypeStruct((4096, 256), BF16),) * 2,
        in_specs=[smem(), pl.BlockSpec((256, 1024), lambda z: (0, z))],
        out_specs=(pl.BlockSpec((512, 256), lambda z: (z, 0)),) * 2,
        compiler_params=pltpu.CompilerParams(vmem_limit_bytes=8 * 2**20),
        cost_estimate=pl.CostEstimate(flops=10**7, bytes_accessed=8 * 2**20, transcendentals=0),
        name="turn",
    )(me, layer)


NQ, NK = 4, 8
SCALE = BLK**-0.5


def key_steps(meta, q_all, g_all, qt, gt, stats, kv, kt, dqt, dkv):
    factor = SCALE * math.log2(math.e)
    dkv[...] = jnp.zeros_like(dkv)

    def chunk(i, first, count, masked):
        keys = count * BLK
        at = [meta[first + n] for n in range(count)]
        rows = [pl.ds(pl.multiple_of(a * BLK, BLK), BLK) for a in at]
        kb = jnp.concatenate([kv[r, :BLK] for r in rows], 0)
        vb = jnp.concatenate([kv[r, BLK:] for r in rows], 0)
        ktb = jnp.concatenate([kt[a] for a in at], 1)
        if masked:
            q_pos = meta[2 * NK + i]
            u = lax.broadcasted_iota(jnp.int32, (BLK, 2 * BLK), 0)
            t = lax.broadcasted_iota(jnp.int32, (BLK, 2 * BLK), 1) % BLK
            ahead = t - u
            visible = [ahead >= (meta[NK + first + n] - q_pos) * BLK for n in range(count)]
        dv = jnp.zeros((keys, BLK), F32)
        dk = jnp.zeros((keys, BLK), F32)
        for pair in range(H // 2):
            cols = slice(pair * 2 * BLK, (pair + 1) * 2 * BLK)
            heads = [slice((2 * pair + g) * BLK, (2 * pair + g + 1) * BLK) for g in range(2)]
            score = jnp.dot(kb, qt[i, :, cols], preferred_element_type=F32)
            prob = jnp.exp2(score * factor - stats[pl.ds(i, 1), cols])
            if masked:
                prob = jnp.concatenate(
                    [
                        jnp.where(visible[n], prob[n * BLK : (n + 1) * BLK], 0.0)
                        for n in range(count)
                    ],
                    0,
                )
            d_prob = jnp.dot(vb, gt[i, :, cols], preferred_element_type=F32)
            d_score = (prob * (d_prob - stats[pl.ds(NQ + i, 1), cols])).astype(BF16)
            g_rows = jnp.concatenate([g_all[i, :, s] for s in heads], 0)
            q_rows = jnp.concatenate([q_all[i, :, s] for s in heads], 0)
            dv = dv + jnp.dot(prob.astype(BF16), g_rows, preferred_element_type=F32)
            dk = dk + jnp.dot(d_score, q_rows, preferred_element_type=F32)
            dqt[i, :, cols] += jnp.dot(ktb, d_score, preferred_element_type=F32)
        for n in range(count):
            dkv[at[n], :, :BLK] += dk[n * BLK : (n + 1) * BLK]
            dkv[at[n], :, BLK:] += dv[n * BLK : (n + 1) * BLK]

    def query_block(i, carry):
        whole = meta[2 * NK + NQ + i]
        pairs = meta[2 * NK + 2 * NQ + i]

        def full_step(j, c):
            chunk(i, 4 * j, 4, False)
            return c

        def pair_step(j, c):
            chunk(i, 4 * whole + 2 * j, 2, True)
            return c

        lax.fori_loop(0, whole, full_step, 0)
        lax.fori_loop(0, pairs, pair_step, 0)
        return carry

    lax.fori_loop(0, NQ, query_block, 0)


def store_keys(dkv, refs):
    for n in range(NK):
        b, i = n // 2, n % 2
        ref = refs[b]
        rows = slice(i * BLK, (i + 1) * BLK)
        ref[rows, :BLK] = (dkv[n, :, :BLK] * SCALE).astype(ref.dtype)
        ref[rows, BLK:] = dkv[n, :, BLK:].astype(ref.dtype)


def first_kernel(meta, *refs):
    q_in, g_in, s_in, kv_in = refs[0:2], refs[2:4], refs[4:6], refs[6:10]
    q_all, g_all, qt, gt, stats, dqt = refs[10:16]
    dkv_out = refs[16]
    kv, kt, dkv, pieces, sems = refs[17:]
    copies = []
    for side in range(2):
        for i in range(2):
            rows = pl.ds(i * BLK, BLK)
            copies.append((q_in[side].at[rows], q_all.at[2 * side + i]))
            copies.append((g_in[side].at[rows], g_all.at[2 * side + i]))
        copies.append((s_in[side], pieces.at[side]))
    for b in range(4):
        source = kv_in[b].at[pl.ds(2 * BLK, 2 * BLK)]
        copies.append((source, kv.at[pl.ds(b * 2 * BLK, 2 * BLK)]))
    copies = [pltpu.make_async_copy(s, d, sems.at[n]) for n, (s, d) in enumerate(copies)]
    for copy in copies:
        copy.start()
    dqt[...] = jnp.zeros_like(dqt)
    for copy in copies:
        copy.wait()
    for side in range(2):
        stats[2 * side : 2 * side + 2, :] = pieces[side, 0:2, :]
        stats[NQ + 2 * side : NQ + 2 * side + 2, :] = pieces[side, 2:4, :]

    def transpose(n, carry):
        for h in range(H):
            cols = slice(h * BLK, (h + 1) * BLK)
            qt[n, :, cols] = q_all[n, :, cols].T
            gt[n, :, cols] = g_all[n, :, cols].T
        return carry

    lax.fori_loop(0, NQ, transpose, 0)
    for n in range(NK):
        kt[n] = kv[n * BLK : (n + 1) * BLK, :BLK].T
    key_steps(meta, q_all, g_all, qt, gt, stats, kv, kt, dqt, dkv)
    store_keys(dkv, [dkv_out.at[pl.ds(b * 2 * BLK, 2 * BLK)] for b in range(4)])


def second_kernel(meta, *refs):
    q_all, g_all, qt, gt, stats, dqt_in = refs[0:6]
    kv_in = refs[6:10]
    dq_own, dq_other = refs[10:12]
    dkv_out = refs[12:16]
    kv, kt, dkv, dqt, sems = refs[16:]
    copies = [
        pltpu.make_async_copy(
            kv_in[b].at[pl.ds(0, 2 * BLK)], kv.at[pl.ds(b * 2 * BLK, 2 * BLK)], sems.at[b]
        )
        for b in range(4)
    ]
    for copy in copies:
        copy.start()
    dqt[...] = dqt_in[...]
    for copy in copies:
        copy.wait()
    for n in range(NK):
        kt[n] = kv[n * BLK : (n + 1) * BLK, :BLK].T
    key_steps(meta, q_all, g_all, qt, gt, stats, kv, kt, dqt, dkv)
    store_keys(dkv, dkv_out)
    for n in range(NQ):
        ref = (dq_own, dq_own, dq_other, dq_other)[n]
        rows = slice(n % 2 * BLK, (n % 2 + 1) * BLK)
        for h in range(H):
            cols = slice(h * BLK, (h + 1) * BLK)
            ref[rows, cols] = (dqt[n, :, cols].T * SCALE).astype(ref.dtype)


WIDE = H * BLK
KEY_SCRATCH = [
    pltpu.VMEM((NK * BLK, 2 * BLK), BF16),
    pltpu.VMEM((NK, BLK, BLK), BF16),
    pltpu.VMEM((NK, BLK, 2 * BLK), F32),
]
COST = pl.CostEstimate(flops=6 * 10**10, bytes_accessed=2**20, transcendentals=2 * 10**6)


def first_call(meta, queries, grads, stats, blocks):
    rows = jax.ShapeDtypeStruct((NQ, BLK, WIDE), BF16)
    return pl.pallas_call(
        first_kernel,
        out_shape=(rows,) * 4
        + (
            jax.ShapeDtypeStruct((2 * NQ, WIDE), F32),
            jax.ShapeDtypeStruct((NQ, BLK, WIDE), F32),
        )
        + (jax.ShapeDtypeStruct((NK * BLK, 2 * BLK), BF16),),
        in_specs=[smem()] + [hbm(), anywhere()] * 2 + [anywhere()] * 6,
        out_specs=(vmem(),) * 7,
        scratch_shapes=KEY_SCRATCH
        + [pltpu.VMEM((2, 8, WIDE), F32), pltpu.SemaphoreType.DMA((14,))],
        compiler_params=pltpu.CompilerParams(vmem_limit_bytes=VMEM_LIMIT),
        cost_estimate=COST,
        name="attention_first",
    )(meta, *queries, *grads, *stats, *blocks)


def second_call(meta, carried, blocks):
    return pl.pallas_call(
        second_kernel,
        out_shape=(
            jax.ShapeDtypeStruct((256, WIDE), F32),
            jax.ShapeDtypeStruct((256, WIDE), BF16),
        )
        + (jax.ShapeDtypeStruct((2 * BLK, 2 * BLK), F32),) * 4,
        in_specs=[smem()] + [vmem()] * 6 + [anywhere()] * 4,
        out_specs=(vmem(),) * 6,
        scratch_shapes=KEY_SCRATCH
        + [pltpu.VMEM((NQ, BLK, WIDE), F32), pltpu.SemaphoreType.DMA((4,))],
        compiler_params=pltpu.CompilerParams(vmem_limit_bytes=VMEM_LIMIT),
        cost_estimate=COST,
        name="attention_second",
    )(meta, *carried, *blocks)


def make_meta(k_pos, q_pos):
    rank = jnp.sum(k_pos[None, :] < k_pos[:, None], axis=1)
    hit = rank[None, :] == jnp.arange(NK)[:, None]
    order = jnp.sum(jnp.where(hit, jnp.arange(NK)[None, :], 0), axis=1)
    ordered = jnp.sum(jnp.where(hit, k_pos[None, :], 0), axis=1)
    below = jnp.sum(k_pos[None, :] < q_pos[:, None], axis=1)
    reached = jnp.sum(k_pos[None, :] <= q_pos[:, None], axis=1)
    whole = below // 4
    pairs = (reached - 4 * whole + 1) // 2
    return jnp.concatenate([order, ordered, q_pos, whole, pairs]).astype(jnp.int32)


def project_kernel(mine_ref, other_ref, g_own, g_other, out_ref):
    def step(z, carry):
        rows = pl.ds(pl.multiple_of(z * 512, 512), 512)
        terms = jnp.dot(mine_ref[rows, :], g_own[...], preferred_element_type=F32) + jnp.dot(
            other_ref[rows, :], g_other[...], preferred_element_type=F32
        )
        at = pl.ds(pl.multiple_of(z * 32, 32), 32)
        out_ref[:, at, :] = terms.astype(BF16).reshape(16, 32, 256)
        return carry

    lax.fori_loop(0, Z, step, 0)


def project(mine, other, g_own, g_other):
    return pl.pallas_call(
        project_kernel,
        out_shape=jax.ShapeDtypeStruct((16, 256, 256), BF16),
        in_specs=[vmem()] * 4,
        out_specs=vmem(),
        compiler_params=pltpu.CompilerParams(vmem_limit_bytes=16 * 2**20),
        cost_estimate=pl.CostEstimate(
            flops=2 * 4096 * 512 * 256, bytes_accessed=8 * 2**20, transcendentals=0
        ),
        name="project",
    )(mine, other, g_own, g_other)


def sum_kernel(place, in_ref, keep_ref, send_ref):
    for j in range(Z // 2):
        for ref, half in ((keep_ref, place[1]), (send_ref, 1 - place[1])):
            at = pl.ds(pl.multiple_of((2 * j + half) * 32, 32), 32)
            value = in_ref[0, at, :].astype(F32)
            for n in range(1, 16):
                value = value + in_ref[n, at, :].astype(F32)
            ref[j * 32 : j * 32 + 32, :] = value.astype(ref.dtype)


def sum_terms(place, terms):
    return pl.pallas_call(
        sum_kernel,
        out_shape=(
            jax.ShapeDtypeStruct((128, 256), F32),
            jax.ShapeDtypeStruct((128, 256), BF16),
        ),
        in_specs=[smem(), vmem()],
        out_specs=(vmem(),) * 2,
        compiler_params=pltpu.CompilerParams(vmem_limit_bytes=8 * 2**20),
        name="sum_terms",
    )(place, terms)


def split_kernel(place, keep_ref, got_ref, *out_refs):
    for k in range(Z // 2):
        at = pl.ds(pl.multiple_of((place[2] + k) % (Z // 2) * 32, 32), 32)
        value = keep_ref[at, :] + got_ref[at, :].astype(F32)
        out_refs[k][...] = value.astype(out_refs[k].dtype)


def split_terms(place, keep, got):
    return pl.pallas_call(
        split_kernel,
        out_shape=(jax.ShapeDtypeStruct((32, 256), F32),)
        + (jax.ShapeDtypeStruct((32, 256), BF16),) * 3,
        in_specs=[smem(), vmem(), vmem()],
        out_specs=(vmem(),) * 4,
        compiler_params=pltpu.CompilerParams(vmem_limit_bytes=4 * 2**20),
        name="split_terms",
    )(place, keep, got)


def body(layer_input, query_rows, key_rows, value_rows, attn_out, d_attn, log_sum_exp, block_order):
    z, x, yh, c = (lax.axis_index(name) for name in ("z", "x", "yh", "c"))
    ctx = (x * YH + yh) * C + c
    place = jnp.stack([c, z % 2, z // 2]).astype(jnp.int32)

    q, g = query_rows[0], d_attn[0]
    pair = jnp.concatenate([key_rows[0], value_rows[0]], axis=1)
    pair_y = fetch(pair, by_ctx(0, 1))
    q_other, g_other = fetch(q, swap_core), fetch(g, swap_core)
    stats = row_stats(attn_out[0], g, log_sum_exp[0])
    stats_other = fetch(stats, swap_core)
    both = jnp.concatenate([pair, pair_y], axis=0)
    blocks = [both] + [fetch(both, by_ctx(k, 0)) for k in ALONG_X[1:]]
    mine, other = turn(place[:1], layer_input[0])

    places = block_order.reshape(16, 2)
    q_pos = jnp.concatenate([places[ctx], places[ctx ^ 1]])

    def owners(row):
        return jnp.concatenate([places[(x + k) % X * 4 + row * 2 + c] for k in ALONG_X])

    blocks, mine, other = lax.optimization_barrier((blocks, mine, other))
    mine_core = fetch(other, swap_core)
    *carried, dkv_y = first_call(
        make_meta(owners(1 - yh), q_pos), (q, q_other), (g, g_other), (stats, stats_other), blocks
    )
    carried, mine_core = lax.optimization_barrier((carried, mine_core))
    dq_own, dq_sent, *dkv = second_call(make_meta(owners(yh), q_pos), carried, blocks)
    dkv_y = fetch(dkv_y, by_ctx(0, 1))
    dkv = [part + dkv_y[256 * b : 256 * b + 256].astype(F32) for b, part in enumerate(dkv)]
    parts = [fetch(part.astype(BF16), by_ctx(-k, 0)) for k, part in zip(ALONG_X[1:], dkv[1:])]
    total = dkv[0]
    for part in parts:
        total = total + part.astype(F32)
    grads = total.astype(BF16)
    grads_core = fetch(grads, swap_core)

    terms = project(mine, mine_core, grads, grads_core)
    terms = lax.all_to_all(terms, ("yl", "x", "yh"), 0, 0)
    terms, dq_sent = lax.optimization_barrier((terms, dq_sent))
    keep, sent = sum_terms(place, terms)
    own, *sent = split_terms(place, keep, fetch(sent, swap_z))
    d_query = (dq_own + fetch(dq_sent, swap_core).astype(F32)).astype(BF16)[None]
    for k in range(1, Z // 2):
        own = own + fetch(sent[k - 1], by_z(-2 * k)).astype(F32)
    return (d_query, own)


def solution(mesh):
    fine = jax.sharding.Mesh(mesh.devices.reshape(Z, YL, X, YH, C), AXES)
    dp, ctx = ("z", "yl"), ("x", "yh", "c")
    rows = P(dp, ctx, None)
    return jax.shard_map(
        body,
        mesh=fine,
        in_specs=(rows, rows, rows, rows, rows, rows, P(dp, None, ctx), P()),
        out_specs=(rows, P(AXES, None)),
        check_vma=False,
    )
```

```python
import math

import jax
import jax.numpy as jnp
from jax import lax
from jax.experimental import pallas as pl
from jax.experimental.pallas import tpu as pltpu
from jax.sharding import PartitionSpec as P

F32 = jnp.float32
BF16 = jnp.bfloat16
BLK = 128
H = 8
Z, YL, X, YH, C = 8, 2, 4, 2, 2
AXES = ("z", "yl", "x", "yh", "c")
VMEM_LIMIT = 24 * 1024 * 1024


def coords(i):
    return (i // 32, i // 16 % 2, i // 4 % 4, i // 2 % 2, i % 2)


def index_of(z, yl, x, yh, c):
    return (((z * YL + yl) * X + x) * YH + yh) * C + c


def fetch(value, shift):
    pairs = [(index_of(*shift(*coords(i))), i) for i in range(Z * YL * X * YH * C)]
    return lax.ppermute(value, AXES, pairs)


def swap_core(z, yl, x, yh, c):
    return (z, yl, x, yh, 1 - c)


def by_ctx(dx, dyh):
    return lambda z, yl, x, yh, c: (z, yl, (x + dx) % X, yh ^ dyh, c)


def by_z(k):
    return lambda z, yl, x, yh, c: ((z + k) % Z, yl, x, yh, c)


def swap_z(z, yl, x, yh, c):
    return (z ^ 1, yl, x, yh, c)


ALONG_X = (0, 1, 3, 2)


def vmem():
    return pl.BlockSpec(memory_space=pltpu.VMEM)


def smem():
    return pl.BlockSpec(memory_space=pltpu.SMEM)


def anywhere():
    return pl.BlockSpec(memory_space=pl.ANY)


def hbm():
    return pl.BlockSpec(memory_space=pltpu.HBM)


def stats_kernel(out_hbm, grad_hbm, lse_hbm, stats_ref, out_ref, grad_ref, lse_ref, sems):
    pairs = ((out_hbm, out_ref), (grad_hbm, grad_ref), (lse_hbm, lse_ref))
    copies = [pltpu.make_async_copy(a, b, sems.at[n]) for n, (a, b) in enumerate(pairs)]
    for copy in copies:
        copy.start()
    stats_ref[4:8, :] = jnp.zeros((4, H * BLK), F32)
    for copy in copies:
        copy.wait()
    for h in range(H):
        cols = slice(h * BLK, (h + 1) * BLK)
        product = out_ref[:, cols].astype(F32) * grad_ref[:, cols].astype(F32)
        delta = jnp.sum(product.T, axis=0, keepdims=True)
        lse2 = lse_ref[h : h + 1, :] * math.log2(math.e)
        for i in range(2):
            rows = slice(i * BLK, (i + 1) * BLK)
            stats_ref[i : i + 1, cols] = lse2[:, rows]
            stats_ref[2 + i : 3 + i, cols] = delta[:, rows]


def row_stats(saved, grad, lse):
    return pl.pallas_call(
        stats_kernel,
        out_shape=jax.ShapeDtypeStruct((8, H * BLK), F32),
        in_specs=[hbm()] * 3,
        out_specs=vmem(),
        scratch_shapes=[
            pltpu.VMEM((256, H * BLK), BF16),
            pltpu.VMEM((256, H * BLK), BF16),
            pltpu.VMEM((H, 256), F32),
            pltpu.SemaphoreType.DMA((3,)),
        ],
        compiler_params=pltpu.CompilerParams(vmem_limit_bytes=8 * 2**20),
        cost_estimate=pl.CostEstimate(flops=10**6, bytes_accessed=2**20, transcendentals=0),
        name="row_stats",
    )(saved, grad, lse)


def turn_kernel(place, x_ref, mine_ref, other_ref, away_ref):
    even = place[0] == 0
    here = lax.rem(pl.program_id(0), 2) == place[1]
    half = pl.multiple_of(lax.div(pl.program_id(0), 2) * 512, 512)
    for u in range(8):
        tile = x_ref[:, u * BLK : (u + 1) * BLK].T
        for yh in range(YH):
            first = tile[yh * 64 : yh * 64 + 32]
            second = tile[yh * 64 + 32 : yh * 64 + 64]
            at = pl.ds(half + (u * 64 + yh * 32), 32)

            def store(a, b):
                @pl.when(here)
                def _():
                    mine_ref[at, :] = a
                    other_ref[at, :] = b

                @pl.when(jnp.logical_not(here))
                def _():
                    away_ref[0, at, :] = a
                    away_ref[1, at, :] = b

            @pl.when(even)
            def _():
                store(first, second)

            @pl.when(jnp.logical_not(even))
            def _():
                store(second, first)


def turn(place, layer):
    half = jax.ShapeDtypeStruct((2048, 256), BF16)
    return pl.pallas_call(
        turn_kernel,
        grid=(Z,),
        out_shape=(half, half, jax.ShapeDtypeStruct((2, 2048, 256), BF16)),
        in_specs=[smem(), pl.BlockSpec((256, 1024), lambda z: (0, z))],
        out_specs=(
            pl.BlockSpec((2048, 256), lambda z: (0, 0)),
            pl.BlockSpec((2048, 256), lambda z: (0, 0)),
            pl.BlockSpec((2, 2048, 256), lambda z: (0, 0, 0)),
        ),
        compiler_params=pltpu.CompilerParams(vmem_limit_bytes=12 * 2**20),
        cost_estimate=pl.CostEstimate(flops=3 * 10**10, bytes_accessed=8 * 2**20, transcendentals=0),
        name="turn",
    )(place, layer)


NQ, NK = 4, 8
SCALE = BLK**-0.5


def key_steps(meta, q_all, g_all, qt, gt, stats, kv, kt, dqt, dkv):
    factor = SCALE * math.log2(math.e)
    dkv[...] = jnp.zeros_like(dkv)

    def chunk(i, first, count, masked):
        at = [meta[first + n] for n in range(count)]
        rows = [pl.ds(pl.multiple_of(a * BLK, BLK), BLK) for a in at]
        kb = jnp.concatenate([kv[r, :BLK] for r in rows], 0)
        vb = jnp.concatenate([kv[r, BLK:] for r in rows], 0)
        ktb = jnp.concatenate([kt[a] for a in at], 1)
        if masked:
            q_pos = meta[2 * NK + i]
            u = lax.broadcasted_iota(jnp.int32, (BLK, 2 * BLK), 0)
            t = lax.broadcasted_iota(jnp.int32, (BLK, 2 * BLK), 1) % BLK
            ahead = t - u
            visible = [ahead >= (meta[NK + first + n] - q_pos) * BLK for n in range(count)]
        def ahead_of(pair):
            cols = slice(pair * 2 * BLK, (pair + 1) * 2 * BLK)
            score = jnp.dot(kb, qt[i, :, cols], preferred_element_type=F32)
            return score, jnp.dot(vb, gt[i, :, cols], preferred_element_type=F32)

        probs, d_scores = [], []
        score, d_prob = ahead_of(0)
        for pair in range(H // 2):
            following = ahead_of(pair + 1) if pair + 1 < H // 2 else (None, None)
            cols = slice(pair * 2 * BLK, (pair + 1) * 2 * BLK)
            prob = jnp.exp2(score * factor - stats[pl.ds(i, 1), cols])
            if masked:
                prob = jnp.concatenate(
                    [
                        jnp.where(visible[n], prob[n * BLK : (n + 1) * BLK], 0.0)
                        for n in range(count)
                    ],
                    0,
                )
            d_scores.append((prob * (d_prob - stats[pl.ds(NQ + i, 1), cols])).astype(BF16))
            probs.append(prob.astype(BF16))
            score, d_prob = following
        prob = jnp.concatenate(probs, 1)
        d_score = jnp.concatenate(d_scores, 1)
        heads = [slice(h * BLK, (h + 1) * BLK) for h in range(H)]
        g_rows = jnp.concatenate([g_all[i, :, s] for s in heads], 0)
        q_rows = jnp.concatenate([q_all[i, :, s] for s in heads], 0)
        dv = jnp.dot(prob, g_rows, preferred_element_type=F32)
        dk = jnp.dot(d_score, q_rows, preferred_element_type=F32)
        dqt[i] += jnp.dot(ktb, d_score, preferred_element_type=F32)
        for n in range(count):
            dkv[at[n], :, :BLK] += dk[n * BLK : (n + 1) * BLK]
            dkv[at[n], :, BLK:] += dv[n * BLK : (n + 1) * BLK]

    def query_block(i, carry):
        whole = meta[2 * NK + NQ + i]
        reached = meta[2 * NK + 2 * NQ + i]
        rest = reached - 4 * whole

        def full_step(j, c):
            chunk(i, 4 * j, 4, False)
            return c

        def pair_step(j, c):
            chunk(i, 4 * whole + 2 * j, 2, True)
            return c

        lax.fori_loop(0, whole, full_step, 0)
        lax.fori_loop(0, lax.div(rest, 2), pair_step, 0)

        @pl.when(lax.rem(rest, 2) == 1)
        def _():
            chunk(i, reached - 1, 1, True)

        return carry

    lax.fori_loop(0, NQ, query_block, 0)


def store_keys(dkv, refs):
    for n in range(NK):
        b, i = n // 2, n % 2
        ref = refs[b]
        rows = slice(i * BLK, (i + 1) * BLK)
        ref[rows, :BLK] = (dkv[n, :, :BLK] * SCALE).astype(ref.dtype)
        ref[rows, BLK:] = dkv[n, :, BLK:].astype(ref.dtype)


def first_kernel(meta, *refs):
    q_in, g_in, s_in, kv_in = refs[0:2], refs[2:4], refs[4:6], refs[6:10]
    q_all, g_all, qt, gt, stats, dqt = refs[10:16]
    dkv_out = refs[16]
    kv, kt, dkv, pieces, sems = refs[17:]
    copies = []
    for side in range(2):
        for i in range(2):
            rows = pl.ds(i * BLK, BLK)
            copies.append((q_in[side].at[rows], q_all.at[2 * side + i]))
            copies.append((g_in[side].at[rows], g_all.at[2 * side + i]))
        copies.append((s_in[side], pieces.at[side]))
    for b in range(4):
        source = kv_in[b].at[pl.ds(2 * BLK, 2 * BLK)]
        copies.append((source, kv.at[pl.ds(b * 2 * BLK, 2 * BLK)]))
    copies = [pltpu.make_async_copy(s, d, sems.at[n]) for n, (s, d) in enumerate(copies)]
    for copy in copies:
        copy.start()
    dqt[...] = jnp.zeros_like(dqt)
    for copy in copies:
        copy.wait()
    for side in range(2):
        stats[2 * side : 2 * side + 2, :] = pieces[side, 0:2, :]
        stats[NQ + 2 * side : NQ + 2 * side + 2, :] = pieces[side, 2:4, :]

    def transpose(n, carry):
        for h in range(H):
            cols = slice(h * BLK, (h + 1) * BLK)
            qt[n, :, cols] = q_all[n, :, cols].T
            gt[n, :, cols] = g_all[n, :, cols].T
        return carry

    lax.fori_loop(0, NQ, transpose, 0)
    for n in range(NK):
        kt[n] = kv[n * BLK : (n + 1) * BLK, :BLK].T
    key_steps(meta, q_all, g_all, qt, gt, stats, kv, kt, dqt, dkv)
    store_keys(dkv, [dkv_out.at[pl.ds(b * 2 * BLK, 2 * BLK)] for b in range(4)])


def second_kernel(meta, *refs):
    q_all, g_all, qt, gt, stats, dqt_in = refs[0:6]
    kv_in = refs[6:10]
    dq_own, dq_other = refs[10:12]
    dkv_out = refs[12:16]
    kv, kt, dkv, dqt, sems = refs[16:]
    copies = [
        pltpu.make_async_copy(
            kv_in[b].at[pl.ds(0, 2 * BLK)], kv.at[pl.ds(b * 2 * BLK, 2 * BLK)], sems.at[b]
        )
        for b in range(4)
    ]
    for copy in copies:
        copy.start()
    dqt[...] = dqt_in[...]
    for copy in copies:
        copy.wait()
    for n in range(NK):
        kt[n] = kv[n * BLK : (n + 1) * BLK, :BLK].T
    key_steps(meta, q_all, g_all, qt, gt, stats, kv, kt, dqt, dkv)
    store_keys(dkv, dkv_out)
    for n in range(NQ):
        ref = (dq_own, dq_own, dq_other, dq_other)[n]
        rows = slice(n % 2 * BLK, (n % 2 + 1) * BLK)
        for h in range(H):
            cols = slice(h * BLK, (h + 1) * BLK)
            ref[rows, cols] = (dqt[n, :, cols].T * SCALE).astype(ref.dtype)


WIDE = H * BLK
KEY_SCRATCH = [
    pltpu.VMEM((NK * BLK, 2 * BLK), BF16),
    pltpu.VMEM((NK, BLK, BLK), BF16),
    pltpu.VMEM((NK, BLK, 2 * BLK), F32),
]
COST = pl.CostEstimate(flops=6 * 10**10, bytes_accessed=2**20, transcendentals=2 * 10**6)


def first_call(meta, queries, grads, stats, blocks):
    rows = jax.ShapeDtypeStruct((NQ, BLK, WIDE), BF16)
    return pl.pallas_call(
        first_kernel,
        out_shape=(rows,) * 4
        + (
            jax.ShapeDtypeStruct((2 * NQ, WIDE), F32),
            jax.ShapeDtypeStruct((NQ, BLK, WIDE), F32),
        )
        + (jax.ShapeDtypeStruct((NK * BLK, 2 * BLK), BF16),),
        in_specs=[smem()] + [hbm(), anywhere()] * 2 + [anywhere()] * 6,
        out_specs=(vmem(),) * 7,
        scratch_shapes=KEY_SCRATCH
        + [pltpu.VMEM((2, 8, WIDE), F32), pltpu.SemaphoreType.DMA((14,))],
        compiler_params=pltpu.CompilerParams(vmem_limit_bytes=VMEM_LIMIT),
        cost_estimate=COST,
        name="attention_first",
    )(meta, *queries, *grads, *stats, *blocks)


def second_call(meta, carried, blocks):
    return pl.pallas_call(
        second_kernel,
        out_shape=(
            jax.ShapeDtypeStruct((256, WIDE), F32),
            jax.ShapeDtypeStruct((256, WIDE), BF16),
        )
        + (jax.ShapeDtypeStruct((2 * BLK, 2 * BLK), F32),) * 4,
        in_specs=[smem()] + [vmem()] * 6 + [anywhere()] * 4,
        out_specs=(vmem(),) * 6,
        scratch_shapes=KEY_SCRATCH
        + [pltpu.VMEM((NQ, BLK, WIDE), F32), pltpu.SemaphoreType.DMA((4,))],
        compiler_params=pltpu.CompilerParams(vmem_limit_bytes=VMEM_LIMIT),
        cost_estimate=COST,
        name="attention_second",
    )(meta, *carried, *blocks)


def make_meta(k_pos, q_pos):
    rank = jnp.sum(k_pos[None, :] < k_pos[:, None], axis=1)
    hit = rank[None, :] == jnp.arange(NK)[:, None]
    order = jnp.sum(jnp.where(hit, jnp.arange(NK)[None, :], 0), axis=1)
    ordered = jnp.sum(jnp.where(hit, k_pos[None, :], 0), axis=1)
    below = jnp.sum(k_pos[None, :] < q_pos[:, None], axis=1)
    reached = jnp.sum(k_pos[None, :] <= q_pos[:, None], axis=1)
    whole = below // 4
    return jnp.concatenate([order, ordered, q_pos, whole, reached]).astype(jnp.int32)


HALF = Z // 2


def project_kernel(a_ref, b_ref, c_ref, d_ref, ga, gb, gc, gd, out_ref):
    def step(j, carry):
        rows = pl.ds(pl.multiple_of(j * 512, 512), 512)
        terms = jnp.dot(a_ref[rows, :], ga[...], preferred_element_type=F32)
        terms = terms + jnp.dot(b_ref[rows, :], gb[...], preferred_element_type=F32)
        terms = terms + jnp.dot(c_ref[0, rows, :], gc[...], preferred_element_type=F32)
        terms = terms + jnp.dot(d_ref[rows, :], gd[...], preferred_element_type=F32)
        at = pl.ds(pl.multiple_of(j * 32, 32), 32)
        out_ref[:, at, :] = terms.astype(BF16).reshape(16, 32, 256)
        return carry

    lax.fori_loop(0, HALF, step, 0)


def project(turned, grads):
    return pl.pallas_call(
        project_kernel,
        out_shape=jax.ShapeDtypeStruct((16, HALF * 32, 256), BF16),
        in_specs=[vmem()] * 8,
        out_specs=vmem(),
        compiler_params=pltpu.CompilerParams(vmem_limit_bytes=12 * 2**20),
        cost_estimate=pl.CostEstimate(
            flops=2 * 4096 * 512 * 256, bytes_accessed=8 * 2**20, transcendentals=0
        ),
        name="project",
    )(*turned, *grads)


def sum_kernel(place, in_ref, own_ref, *out_refs):
    for k in range(HALF):
        at = pl.ds(pl.multiple_of((place[2] + k) % HALF * 32, 32), 32)
        value = in_ref[0, at, :].astype(F32)
        for j in range(1, 16):
            value = value + in_ref[j, at, :].astype(F32)
        ref = own_ref if k == 0 else out_refs[k - 1]
        ref[...] = value.astype(ref.dtype)


def sum_terms(place, terms):
    return pl.pallas_call(
        sum_kernel,
        out_shape=(jax.ShapeDtypeStruct((32, 256), F32),)
        + (jax.ShapeDtypeStruct((32, 256), BF16),) * (HALF - 1),
        in_specs=[smem(), vmem()],
        out_specs=(vmem(),) * HALF,
        compiler_params=pltpu.CompilerParams(vmem_limit_bytes=8 * 2**20),
        name="sum_terms",
    )(place, terms)


def body(layer_input, query_rows, key_rows, value_rows, attn_out, d_attn, log_sum_exp, block_order):
    z, x, yh, c = (lax.axis_index(name) for name in ("z", "x", "yh", "c"))
    ctx = (x * YH + yh) * C + c
    place = jnp.stack([c, z % 2, z // 2]).astype(jnp.int32)

    q, g = query_rows[0], d_attn[0]
    pair = jnp.concatenate([key_rows[0], value_rows[0]], axis=1)
    pair_y = fetch(pair, by_ctx(0, 1))
    q_other, g_other = fetch(q, swap_core), fetch(g, swap_core)
    stats = row_stats(attn_out[0], g, log_sum_exp[0])
    stats_other = fetch(stats, swap_core)
    both = jnp.concatenate([pair, pair_y], axis=0)
    blocks = [both] + [fetch(both, by_ctx(k, 0)) for k in ALONG_X[1:]]
    mine, other, away = turn(place, layer_input[0])

    places = block_order.reshape(16, 2)
    q_pos = jnp.concatenate([places[ctx], places[ctx ^ 1]])

    def owners(row):
        return jnp.concatenate([places[(x + k) % X * 4 + row * 2 + c] for k in ALONG_X])

    blocks, mine, other, away = lax.optimization_barrier((blocks, mine, other, away))
    away = fetch(away, swap_z)
    mine_core = fetch(other, swap_core)
    *carried, dkv_y = first_call(
        make_meta(owners(1 - yh), q_pos), (q, q_other), (g, g_other), (stats, stats_other), blocks
    )
    carried, mine_core = lax.optimization_barrier((carried, mine_core))
    carried, mine_core = lax.optimization_barrier((carried, mine_core))
    dq_own, dq_sent, *dkv = second_call(make_meta(owners(yh), q_pos), carried, blocks)
    dkv_y = fetch(dkv_y, by_ctx(0, 1))
    dkv = [part + dkv_y[256 * b : 256 * b + 256].astype(F32) for b, part in enumerate(dkv)]
    parts = [fetch(part.astype(BF16), by_ctx(-k, 0)) for k, part in zip(ALONG_X[1:], dkv[1:])]
    total = dkv[0]
    for part in parts:
        total = total + part.astype(F32)
    grads = total.astype(BF16)
    grads_z = fetch(grads, swap_z)
    away, grads_core = lax.optimization_barrier((away, fetch(grads, swap_core)))
    grads_zc = fetch(grads_z, swap_core)
    mine_zc = fetch(away[1], swap_core)

    terms = project((mine, mine_core, away, mine_zc), (grads, grads_core, grads_z, grads_zc))
    terms = lax.all_to_all(terms, ("yl", "x", "yh"), 0, 0)
    terms, dq_sent = lax.optimization_barrier((terms, dq_sent))
    own, *sent = sum_terms(place, terms)
    d_query = (dq_own + fetch(dq_sent, swap_core).astype(F32)).astype(BF16)[None]
    for k in range(1, HALF):
        own = own + fetch(sent[k - 1], by_z(-2 * k)).astype(F32)
    return (d_query, own)


def solution(mesh):
    fine = jax.sharding.Mesh(mesh.devices.reshape(Z, YL, X, YH, C), AXES)
    dp, ctx = ("z", "yl"), ("x", "yh", "c")
    rows = P(dp, ctx, None)
    return jax.shard_map(
        body,
        mesh=fine,
        in_specs=(rows, rows, rows, rows, rows, rows, P(dp, None, ctx), P()),
        out_specs=(rows, P(AXES, None)),
        check_vma=False,
    )
```

```python
import math

import jax
import jax.numpy as jnp
from jax import lax
from jax.experimental import pallas as pl
from jax.experimental.pallas import tpu as pltpu
from jax.sharding import PartitionSpec as P

F32 = jnp.float32
BF16 = jnp.bfloat16
BLK = 128
H = 8
Z, YL, X, YH, C = 8, 2, 4, 2, 2
AXES = ("z", "yl", "x", "yh", "c")
VMEM_LIMIT = 24 * 1024 * 1024


def coords(i):
    return (i // 32, i // 16 % 2, i // 4 % 4, i // 2 % 2, i % 2)


def index_of(z, yl, x, yh, c):
    return (((z * YL + yl) * X + x) * YH + yh) * C + c


def fetch(value, shift):
    pairs = [(index_of(*shift(*coords(i))), i) for i in range(Z * YL * X * YH * C)]
    return lax.ppermute(value, AXES, pairs)


def swap_core(z, yl, x, yh, c):
    return (z, yl, x, yh, 1 - c)


def by_ctx(dx, dyh):
    return lambda z, yl, x, yh, c: (z, yl, (x + dx) % X, yh ^ dyh, c)


def by_z(k):
    return lambda z, yl, x, yh, c: ((z + k) % Z, yl, x, yh, c)


def swap_z(z, yl, x, yh, c):
    return (z ^ 1, yl, x, yh, c)


ALONG_X = (0, 1, 3, 2)


def vmem():
    return pl.BlockSpec(memory_space=pltpu.VMEM)


def smem():
    return pl.BlockSpec(memory_space=pltpu.SMEM)


def anywhere():
    return pl.BlockSpec(memory_space=pl.ANY)


def hbm():
    return pl.BlockSpec(memory_space=pltpu.HBM)


def stats_kernel(out_hbm, grad_hbm, lse_hbm, stats_ref, out_ref, grad_ref, lse_ref, sems):
    pairs = ((out_hbm, out_ref), (grad_hbm, grad_ref), (lse_hbm, lse_ref))
    copies = [pltpu.make_async_copy(a, b, sems.at[n]) for n, (a, b) in enumerate(pairs)]
    for copy in copies:
        copy.start()
    stats_ref[4:8, :] = jnp.zeros((4, H * BLK), F32)
    for copy in copies:
        copy.wait()
    for h in range(H):
        cols = slice(h * BLK, (h + 1) * BLK)
        product = out_ref[:, cols].astype(F32) * grad_ref[:, cols].astype(F32)
        delta = jnp.sum(product.T, axis=0, keepdims=True)
        lse2 = lse_ref[h : h + 1, :] * math.log2(math.e)
        for i in range(2):
            rows = slice(i * BLK, (i + 1) * BLK)
            stats_ref[i : i + 1, cols] = lse2[:, rows]
            stats_ref[2 + i : 3 + i, cols] = delta[:, rows]


def row_stats(saved, grad, lse):
    return pl.pallas_call(
        stats_kernel,
        out_shape=jax.ShapeDtypeStruct((8, H * BLK), F32),
        in_specs=[hbm()] * 3,
        out_specs=vmem(),
        scratch_shapes=[
            pltpu.VMEM((256, H * BLK), BF16),
            pltpu.VMEM((256, H * BLK), BF16),
            pltpu.VMEM((H, 256), F32),
            pltpu.SemaphoreType.DMA((3,)),
        ],
        compiler_params=pltpu.CompilerParams(vmem_limit_bytes=8 * 2**20),
        cost_estimate=pl.CostEstimate(flops=10**6, bytes_accessed=2**20, transcendentals=0),
        name="row_stats",
    )(saved, grad, lse)


def turn_kernel(place, x_ref, mine_ref, other_ref, away_ref):
    even = place[0] == 0
    here = lax.rem(pl.program_id(0), 2) == place[1]
    half = pl.multiple_of(lax.div(pl.program_id(0), 2) * 512, 512)
    for u in range(8):
        tile = x_ref[:, u * BLK : (u + 1) * BLK].T
        for yh in range(YH):
            first = tile[yh * 64 : yh * 64 + 32]
            second = tile[yh * 64 + 32 : yh * 64 + 64]
            at = pl.ds(half + (u * 64 + yh * 32), 32)

            def store(a, b):
                @pl.when(here)
                def _():
                    mine_ref[at, :] = a
                    other_ref[at, :] = b

                @pl.when(jnp.logical_not(here))
                def _():
                    away_ref[0, at, :] = a
                    away_ref[1, at, :] = b

            @pl.when(even)
            def _():
                store(first, second)

            @pl.when(jnp.logical_not(even))
            def _():
                store(second, first)


def turn(place, layer):
    half = jax.ShapeDtypeStruct((2048, 256), BF16)
    return pl.pallas_call(
        turn_kernel,
        grid=(Z,),
        out_shape=(half, half, jax.ShapeDtypeStruct((2, 2048, 256), BF16)),
        in_specs=[smem(), pl.BlockSpec((256, 1024), lambda z: (0, z))],
        out_specs=(
            pl.BlockSpec((2048, 256), lambda z: (0, 0)),
            pl.BlockSpec((2048, 256), lambda z: (0, 0)),
            pl.BlockSpec((2, 2048, 256), lambda z: (0, 0, 0)),
        ),
        compiler_params=pltpu.CompilerParams(vmem_limit_bytes=12 * 2**20),
        cost_estimate=pl.CostEstimate(flops=10**7, bytes_accessed=8 * 2**20, transcendentals=0),
        name="turn",
    )(place, layer)


NQ, NK = 4, 8
SCALE = BLK**-0.5


def key_steps(meta, q_all, g_all, qt, gt, stats, kv, kt, dqt, dkv):
    factor = SCALE * math.log2(math.e)
    dkv[...] = jnp.zeros_like(dkv)

    def chunk(i, first, count, masked):
        at = [meta[first + n] for n in range(count)]
        rows = [pl.ds(pl.multiple_of(a * BLK, BLK), BLK) for a in at]
        kb = jnp.concatenate([kv[r, :BLK] for r in rows], 0)
        vb = jnp.concatenate([kv[r, BLK:] for r in rows], 0)
        ktb = jnp.concatenate([kt[a] for a in at], 1)
        if masked:
            q_pos = meta[2 * NK + i]
            u = lax.broadcasted_iota(jnp.int32, (BLK, 2 * BLK), 0)
            t = lax.broadcasted_iota(jnp.int32, (BLK, 2 * BLK), 1) % BLK
            ahead = t - u
            visible = [ahead >= (meta[NK + first + n] - q_pos) * BLK for n in range(count)]
        def ahead_of(pair):
            cols = slice(pair * 2 * BLK, (pair + 1) * 2 * BLK)
            score = jnp.dot(kb, qt[i, :, cols], preferred_element_type=F32)
            return score, jnp.dot(vb, gt[i, :, cols], preferred_element_type=F32)

        probs, d_scores = [], []
        score, d_prob = ahead_of(0)
        for pair in range(H // 2):
            following = ahead_of(pair + 1) if pair + 1 < H // 2 else (None, None)
            cols = slice(pair * 2 * BLK, (pair + 1) * 2 * BLK)
            prob = jnp.exp2(score * factor - stats[pl.ds(i, 1), cols])
            if masked:
                prob = jnp.concatenate(
                    [
                        jnp.where(visible[n], prob[n * BLK : (n + 1) * BLK], 0.0)
                        for n in range(count)
                    ],
                    0,
                )
            d_scores.append((prob * (d_prob - stats[pl.ds(NQ + i, 1), cols])).astype(BF16))
            probs.append(prob.astype(BF16))
            score, d_prob = following
        prob = jnp.concatenate(probs, 1)
        d_score = jnp.concatenate(d_scores, 1)
        heads = [slice(h * BLK, (h + 1) * BLK) for h in range(H)]
        g_rows = jnp.concatenate([g_all[i, :, s] for s in heads], 0)
        q_rows = jnp.concatenate([q_all[i, :, s] for s in heads], 0)
        dv = jnp.dot(prob, g_rows, preferred_element_type=F32)
        dk = jnp.dot(d_score, q_rows, preferred_element_type=F32)
        dqt[i] += jnp.dot(ktb, d_score, preferred_element_type=F32)
        for n in range(count):
            dkv[at[n], :, :BLK] += dk[n * BLK : (n + 1) * BLK]
            dkv[at[n], :, BLK:] += dv[n * BLK : (n + 1) * BLK]

    def query_block(i, carry):
        whole = meta[2 * NK + NQ + i]
        reached = meta[2 * NK + 2 * NQ + i]
        rest = reached - 4 * whole

        def full_step(j, c):
            chunk(i, 4 * j, 4, False)
            return c

        def pair_step(j, c):
            chunk(i, 4 * whole + 2 * j, 2, True)
            return c

        lax.fori_loop(0, whole, full_step, 0)
        lax.fori_loop(0, lax.div(rest, 2), pair_step, 0)

        @pl.when(lax.rem(rest, 2) == 1)
        def _():
            chunk(i, reached - 1, 1, True)

        return carry

    lax.fori_loop(0, NQ, query_block, 0)


def store_keys(dkv, refs):
    for n in range(NK):
        b, i = n // 2, n % 2
        ref = refs[b]
        rows = slice(i * BLK, (i + 1) * BLK)
        ref[rows, :BLK] = (dkv[n, :, :BLK] * SCALE).astype(ref.dtype)
        ref[rows, BLK:] = dkv[n, :, BLK:].astype(ref.dtype)


def first_kernel(meta, *refs):
    q_in, g_in, s_in, kv_in = refs[0:2], refs[2:4], refs[4:6], refs[6:10]
    q_all, g_all, qt, gt, stats, dqt = refs[10:16]
    dkv_out = refs[16]
    kv, kt, dkv, pieces, sems = refs[17:]
    copies = []
    for side in range(2):
        for i in range(2):
            rows = pl.ds(i * BLK, BLK)
            copies.append((q_in[side].at[rows], q_all.at[2 * side + i]))
            copies.append((g_in[side].at[rows], g_all.at[2 * side + i]))
        copies.append((s_in[side], pieces.at[side]))
    for b in range(4):
        source = kv_in[b].at[pl.ds(2 * BLK, 2 * BLK)]
        copies.append((source, kv.at[pl.ds(b * 2 * BLK, 2 * BLK)]))
    copies = [pltpu.make_async_copy(s, d, sems.at[n]) for n, (s, d) in enumerate(copies)]
    for copy in copies:
        copy.start()
    dqt[...] = jnp.zeros_like(dqt)
    for copy in copies:
        copy.wait()
    for side in range(2):
        stats[2 * side : 2 * side + 2, :] = pieces[side, 0:2, :]
        stats[NQ + 2 * side : NQ + 2 * side + 2, :] = pieces[side, 2:4, :]

    def transpose(n, carry):
        for h in range(H):
            cols = slice(h * BLK, (h + 1) * BLK)
            qt[n, :, cols] = q_all[n, :, cols].T
            gt[n, :, cols] = g_all[n, :, cols].T
        return carry

    lax.fori_loop(0, NQ, transpose, 0)
    for n in range(NK):
        kt[n] = kv[n * BLK : (n + 1) * BLK, :BLK].T
    key_steps(meta, q_all, g_all, qt, gt, stats, kv, kt, dqt, dkv)
    store_keys(dkv, [dkv_out.at[pl.ds(b * 2 * BLK, 2 * BLK)] for b in range(4)])


def second_kernel(meta, *refs):
    q_all, g_all, qt, gt, stats, dqt_in = refs[0:6]
    kv_in = refs[6:10]
    dq_own, dq_other = refs[10:12]
    dkv_out = refs[12:16]
    kv, kt, dkv, dqt, sems = refs[16:]
    copies = [
        pltpu.make_async_copy(
            kv_in[b].at[pl.ds(0, 2 * BLK)], kv.at[pl.ds(b * 2 * BLK, 2 * BLK)], sems.at[b]
        )
        for b in range(4)
    ]
    for copy in copies:
        copy.start()
    dqt[...] = dqt_in[...]
    for copy in copies:
        copy.wait()
    for n in range(NK):
        kt[n] = kv[n * BLK : (n + 1) * BLK, :BLK].T
    key_steps(meta, q_all, g_all, qt, gt, stats, kv, kt, dqt, dkv)
    store_keys(dkv, dkv_out)
    for n in range(NQ):
        ref = (dq_own, dq_own, dq_other, dq_other)[n]
        rows = slice(n % 2 * BLK, (n % 2 + 1) * BLK)
        for h in range(H):
            cols = slice(h * BLK, (h + 1) * BLK)
            ref[rows, cols] = (dqt[n, :, cols].T * SCALE).astype(ref.dtype)


WIDE = H * BLK
KEY_SCRATCH = [
    pltpu.VMEM((NK * BLK, 2 * BLK), BF16),
    pltpu.VMEM((NK, BLK, BLK), BF16),
    pltpu.VMEM((NK, BLK, 2 * BLK), F32),
]
COST = pl.CostEstimate(flops=6 * 10**9, bytes_accessed=2**20, transcendentals=2 * 10**6)


def first_call(meta, queries, grads, stats, blocks):
    rows = jax.ShapeDtypeStruct((NQ, BLK, WIDE), BF16)
    return pl.pallas_call(
        first_kernel,
        out_shape=(rows,) * 4
        + (
            jax.ShapeDtypeStruct((2 * NQ, WIDE), F32),
            jax.ShapeDtypeStruct((NQ, BLK, WIDE), F32),
        )
        + (jax.ShapeDtypeStruct((NK * BLK, 2 * BLK), BF16),),
        in_specs=[smem()] + [hbm(), anywhere()] * 2 + [anywhere()] * 6,
        out_specs=(vmem(),) * 7,
        scratch_shapes=KEY_SCRATCH
        + [pltpu.VMEM((2, 8, WIDE), F32), pltpu.SemaphoreType.DMA((14,))],
        compiler_params=pltpu.CompilerParams(vmem_limit_bytes=VMEM_LIMIT),
        cost_estimate=COST,
        name="attention_first",
    )(meta, *queries, *grads, *stats, *blocks)


def second_call(meta, carried, blocks):
    return pl.pallas_call(
        second_kernel,
        out_shape=(
            jax.ShapeDtypeStruct((256, WIDE), F32),
            jax.ShapeDtypeStruct((256, WIDE), BF16),
        )
        + (jax.ShapeDtypeStruct((2 * BLK, 2 * BLK), F32),) * 4,
        in_specs=[smem()] + [vmem()] * 6 + [anywhere()] * 4,
        out_specs=(vmem(),) * 6,
        scratch_shapes=KEY_SCRATCH
        + [pltpu.VMEM((NQ, BLK, WIDE), F32), pltpu.SemaphoreType.DMA((4,))],
        compiler_params=pltpu.CompilerParams(vmem_limit_bytes=VMEM_LIMIT),
        cost_estimate=COST,
        name="attention_second",
    )(meta, *carried, *blocks)


def make_meta(k_pos, q_pos):
    rank = jnp.sum(k_pos[None, :] < k_pos[:, None], axis=1)
    hit = rank[None, :] == jnp.arange(NK)[:, None]
    order = jnp.sum(jnp.where(hit, jnp.arange(NK)[None, :], 0), axis=1)
    ordered = jnp.sum(jnp.where(hit, k_pos[None, :], 0), axis=1)
    below = jnp.sum(k_pos[None, :] < q_pos[:, None], axis=1)
    reached = jnp.sum(k_pos[None, :] <= q_pos[:, None], axis=1)
    whole = below // 4
    return jnp.concatenate([order, ordered, q_pos, whole, reached]).astype(jnp.int32)


HALF = Z // 2


def project_kernel(a_ref, b_ref, c_ref, d_ref, ga, gb, gc, gd, out_ref):
    def step(j, carry):
        rows = pl.ds(pl.multiple_of(j * 512, 512), 512)
        terms = jnp.dot(a_ref[rows, :], ga[...], preferred_element_type=F32)
        terms = terms + jnp.dot(b_ref[rows, :], gb[...], preferred_element_type=F32)
        terms = terms + jnp.dot(c_ref[0, rows, :], gc[...], preferred_element_type=F32)
        terms = terms + jnp.dot(d_ref[rows, :], gd[...], preferred_element_type=F32)
        at = pl.ds(pl.multiple_of(j * 32, 32), 32)
        out_ref[:, at, :] = terms.astype(BF16).reshape(16, 32, 256)
        return carry

    lax.fori_loop(0, HALF, step, 0)


def project(turned, grads):
    return pl.pallas_call(
        project_kernel,
        out_shape=jax.ShapeDtypeStruct((16, HALF * 32, 256), BF16),
        in_specs=[vmem()] * 8,
        out_specs=vmem(),
        compiler_params=pltpu.CompilerParams(vmem_limit_bytes=12 * 2**20),
        cost_estimate=pl.CostEstimate(
            flops=2 * 4096 * 512 * 256, bytes_accessed=8 * 2**20, transcendentals=0
        ),
        name="project",
    )(*turned, *grads)


def sum_kernel(place, in_ref, own_ref, *out_refs):
    for k in range(HALF):
        at = pl.ds(pl.multiple_of((place[2] + k) % HALF * 32, 32), 32)
        value = in_ref[0, at, :].astype(F32)
        for j in range(1, 16):
            value = value + in_ref[j, at, :].astype(F32)
        ref = own_ref if k == 0 else out_refs[k - 1]
        ref[...] = value.astype(ref.dtype)


def sum_terms(place, terms):
    return pl.pallas_call(
        sum_kernel,
        out_shape=(jax.ShapeDtypeStruct((32, 256), F32),)
        + (jax.ShapeDtypeStruct((32, 256), BF16),) * (HALF - 1),
        in_specs=[smem(), vmem()],
        out_specs=(vmem(),) * HALF,
        compiler_params=pltpu.CompilerParams(vmem_limit_bytes=8 * 2**20),
        name="sum_terms",
    )(place, terms)


def body(layer_input, query_rows, key_rows, value_rows, attn_out, d_attn, log_sum_exp, block_order):
    z, x, yh, c = (lax.axis_index(name) for name in ("z", "x", "yh", "c"))
    ctx = (x * YH + yh) * C + c
    place = jnp.stack([c, z % 2, z // 2]).astype(jnp.int32)

    q, g = query_rows[0], d_attn[0]
    pair = jnp.concatenate([key_rows[0], value_rows[0]], axis=1)
    pair_y = fetch(pair, by_ctx(0, 1))
    q_other, g_other = fetch(q, swap_core), fetch(g, swap_core)
    stats = row_stats(attn_out[0], g, log_sum_exp[0])
    stats_other = fetch(stats, swap_core)
    pair_y, q_other, g_other = lax.optimization_barrier((pair_y, q_other, g_other))
    both = jnp.concatenate([pair, pair_y], axis=0)
    blocks = [both] + [fetch(both, by_ctx(k, 0)) for k in ALONG_X[1:]]
    mine, other, away = turn(place, layer_input[0])

    places = block_order.reshape(16, 2)
    q_pos = jnp.concatenate([places[ctx], places[ctx ^ 1]])

    def owners(row):
        return jnp.concatenate([places[(x + k) % X * 4 + row * 2 + c] for k in ALONG_X])

    away = fetch(away, swap_z)
    mine_core = fetch(other, swap_core)
    blocks, mine = lax.optimization_barrier((blocks, mine))
    *carried, dkv_y = first_call(
        make_meta(owners(1 - yh), q_pos), (q, q_other), (g, g_other), (stats, stats_other), blocks
    )
    carried, mine_core = lax.optimization_barrier((carried, mine_core))
    carried, mine_core = lax.optimization_barrier((carried, mine_core))
    dq_own, dq_sent, *dkv = second_call(make_meta(owners(yh), q_pos), carried, blocks)
    dkv_y = fetch(dkv_y, by_ctx(0, 1))
    dkv = [part + dkv_y[256 * b : 256 * b + 256].astype(F32) for b, part in enumerate(dkv)]
    parts = [fetch(part.astype(BF16), by_ctx(-k, 0)) for k, part in zip(ALONG_X[1:], dkv[1:])]
    total = dkv[0]
    for part in parts:
        total = total + part.astype(F32)
    grads = total.astype(BF16)
    grads_z = fetch(grads, swap_z)
    away, grads_core = lax.optimization_barrier((away, fetch(grads, swap_core)))
    grads_zc = fetch(grads_z, swap_core)
    mine_zc = fetch(away[1], swap_core)

    terms = project((mine, mine_core, away, mine_zc), (grads, grads_core, grads_z, grads_zc))
    terms = lax.all_to_all(terms, ("yl", "x", "yh"), 0, 0)
    terms, dq_sent = lax.optimization_barrier((terms, dq_sent))
    own, *sent = sum_terms(place, terms)
    d_query = (dq_own + fetch(dq_sent, swap_core).astype(F32)).astype(BF16)[None]
    for k in range(1, HALF):
        own = own + fetch(sent[k - 1], by_z(-2 * k)).astype(F32)
    return (d_query, own)


def solution(mesh):
    fine = jax.sharding.Mesh(mesh.devices.reshape(Z, YL, X, YH, C), AXES)
    dp, ctx = ("z", "yl"), ("x", "yh", "c")
    rows = P(dp, ctx, None)
    return jax.shard_map(
        body,
        mesh=fine,
        in_specs=(rows, rows, rows, rows, rows, rows, P(dp, None, ctx), P()),
        out_specs=(rows, P(AXES, None)),
        check_vma=False,
    )
```

```python
import math

import jax
import jax.numpy as jnp
from jax import lax
from jax.experimental import pallas as pl
from jax.experimental.pallas import tpu as pltpu
from jax.sharding import PartitionSpec as P

F32 = jnp.float32
BF16 = jnp.bfloat16
BLK = 128
H = 8
Z, YL, X, YH, C = 8, 2, 4, 2, 2
AXES = ("z", "yl", "x", "yh", "c")
VMEM_LIMIT = 24 * 1024 * 1024


def coords(i):
    return (i // 32, i // 16 % 2, i // 4 % 4, i // 2 % 2, i % 2)


def index_of(z, yl, x, yh, c):
    return (((z * YL + yl) * X + x) * YH + yh) * C + c


def fetch(value, shift):
    pairs = [(index_of(*shift(*coords(i))), i) for i in range(Z * YL * X * YH * C)]
    return lax.ppermute(value, AXES, pairs)


def swap_core(z, yl, x, yh, c):
    return (z, yl, x, yh, 1 - c)


def by_ctx(dx, dyh):
    return lambda z, yl, x, yh, c: (z, yl, (x + dx) % X, yh ^ dyh, c)


def by_z(k):
    return lambda z, yl, x, yh, c: ((z + k) % Z, yl, x, yh, c)


def swap_z(z, yl, x, yh, c):
    return (z ^ 1, yl, x, yh, c)


ALONG_X = (0, 1, 3, 2)


def vmem():
    return pl.BlockSpec(memory_space=pltpu.VMEM)


def smem():
    return pl.BlockSpec(memory_space=pltpu.SMEM)


def anywhere():
    return pl.BlockSpec(memory_space=pl.ANY)


def hbm():
    return pl.BlockSpec(memory_space=pltpu.HBM)


def stats_kernel(out_hbm, grad_hbm, lse_hbm, stats_ref, out_ref, grad_ref, lse_ref, sems):
    pairs = ((out_hbm, out_ref), (grad_hbm, grad_ref), (lse_hbm, lse_ref))
    copies = [pltpu.make_async_copy(a, b, sems.at[n]) for n, (a, b) in enumerate(pairs)]
    for copy in copies:
        copy.start()
    stats_ref[4:8, :] = jnp.zeros((4, H * BLK), F32)
    for copy in copies:
        copy.wait()
    for h in range(H):
        cols = slice(h * BLK, (h + 1) * BLK)
        product = out_ref[:, cols].astype(F32) * grad_ref[:, cols].astype(F32)
        delta = jnp.sum(product.T, axis=0, keepdims=True)
        lse2 = lse_ref[h : h + 1, :] * math.log2(math.e)
        for i in range(2):
            rows = slice(i * BLK, (i + 1) * BLK)
            stats_ref[i : i + 1, cols] = lse2[:, rows]
            stats_ref[2 + i : 3 + i, cols] = delta[:, rows]


def row_stats(saved, grad, lse):
    return pl.pallas_call(
        stats_kernel,
        out_shape=jax.ShapeDtypeStruct((8, H * BLK), F32),
        in_specs=[hbm()] * 3,
        out_specs=vmem(),
        scratch_shapes=[
            pltpu.VMEM((256, H * BLK), BF16),
            pltpu.VMEM((256, H * BLK), BF16),
            pltpu.VMEM((H, 256), F32),
            pltpu.SemaphoreType.DMA((3,)),
        ],
        compiler_params=pltpu.CompilerParams(vmem_limit_bytes=8 * 2**20),
        cost_estimate=pl.CostEstimate(flops=10**6, bytes_accessed=2**20, transcendentals=0),
        name="row_stats",
    )(saved, grad, lse)


def turn_kernel(place, x_ref, mine_ref, other_ref, away_ref):
    even = place[0] == 0
    here = lax.rem(pl.program_id(0), 2) == place[1]
    half = pl.multiple_of(lax.div(pl.program_id(0), 2) * 512, 512)
    for u in range(8):
        tile = x_ref[:, u * BLK : (u + 1) * BLK].T
        for yh in range(YH):
            first = tile[yh * 64 : yh * 64 + 32]
            second = tile[yh * 64 + 32 : yh * 64 + 64]
            at = pl.ds(half + (u * 64 + yh * 32), 32)

            def store(a, b):
                @pl.when(here)
                def _():
                    mine_ref[at, :] = a
                    other_ref[at, :] = b

                @pl.when(jnp.logical_not(here))
                def _():
                    away_ref[0, at, :] = a
                    away_ref[1, at, :] = b

            @pl.when(even)
            def _():
                store(first, second)

            @pl.when(jnp.logical_not(even))
            def _():
                store(second, first)


def turn(place, layer):
    half = jax.ShapeDtypeStruct((2048, 256), BF16)
    return pl.pallas_call(
        turn_kernel,
        grid=(Z,),
        out_shape=(half, half, jax.ShapeDtypeStruct((2, 2048, 256), BF16)),
        in_specs=[smem(), pl.BlockSpec((256, 1024), lambda z: (0, z))],
        out_specs=(
            pl.BlockSpec((2048, 256), lambda z: (0, 0)),
            pl.BlockSpec((2048, 256), lambda z: (0, 0)),
            pl.BlockSpec((2, 2048, 256), lambda z: (0, 0, 0)),
        ),
        compiler_params=pltpu.CompilerParams(vmem_limit_bytes=12 * 2**20),
        cost_estimate=pl.CostEstimate(flops=10**9, bytes_accessed=8 * 2**20, transcendentals=0),
        name="turn",
    )(place, layer)


NQ, NK = 4, 8
SCALE = BLK**-0.5


def key_steps(meta, q_all, g_all, qt, gt, stats, kv, kt, dqt, dkv):
    factor = SCALE * math.log2(math.e)
    dkv[...] = jnp.zeros_like(dkv)

    def chunk(i, first, count, masked):
        at = [meta[first + n] for n in range(count)]
        rows = [pl.ds(pl.multiple_of(a * BLK, BLK), BLK) for a in at]
        kb = jnp.concatenate([kv[r, :BLK] for r in rows], 0)
        vb = jnp.concatenate([kv[r, BLK:] for r in rows], 0)
        ktb = jnp.concatenate([kt[a] for a in at], 1)
        if masked:
            q_pos = meta[2 * NK + i]
            u = lax.broadcasted_iota(jnp.int32, (BLK, 2 * BLK), 0)
            t = lax.broadcasted_iota(jnp.int32, (BLK, 2 * BLK), 1) % BLK
            ahead = t - u
            visible = [ahead >= (meta[NK + first + n] - q_pos) * BLK for n in range(count)]
        def ahead_of(pair):
            cols = slice(pair * 2 * BLK, (pair + 1) * 2 * BLK)
            score = jnp.dot(kb, qt[i, :, cols], preferred_element_type=F32)
            return score, jnp.dot(vb, gt[i, :, cols], preferred_element_type=F32)

        probs, d_scores = [], []
        score, d_prob = ahead_of(0)
        for pair in range(H // 2):
            following = ahead_of(pair + 1) if pair + 1 < H // 2 else (None, None)
            cols = slice(pair * 2 * BLK, (pair + 1) * 2 * BLK)
            prob = jnp.exp2(score * factor - stats[pl.ds(i, 1), cols])
            if masked:
                prob = jnp.concatenate(
                    [
                        jnp.where(visible[n], prob[n * BLK : (n + 1) * BLK], 0.0)
                        for n in range(count)
                    ],
                    0,
                )
            d_scores.append((prob * (d_prob - stats[pl.ds(NQ + i, 1), cols])).astype(BF16))
            probs.append(prob.astype(BF16))
            score, d_prob = following
        prob = jnp.concatenate(probs, 1)
        d_score = jnp.concatenate(d_scores, 1)
        heads = [slice(h * BLK, (h + 1) * BLK) for h in range(H)]
        g_rows = jnp.concatenate([g_all[i, :, s] for s in heads], 0)
        q_rows = jnp.concatenate([q_all[i, :, s] for s in heads], 0)
        dv = jnp.dot(prob, g_rows, preferred_element_type=F32)
        dk = jnp.dot(d_score, q_rows, preferred_element_type=F32)
        dqt[i] += jnp.dot(ktb, d_score, preferred_element_type=F32)
        for n in range(count):
            dkv[at[n], :, :BLK] += dk[n * BLK : (n + 1) * BLK]
            dkv[at[n], :, BLK:] += dv[n * BLK : (n + 1) * BLK]

    def query_block(i, carry):
        whole = meta[2 * NK + NQ + i]
        reached = meta[2 * NK + 2 * NQ + i]
        rest = reached - 4 * whole

        def full_step(j, c):
            chunk(i, 4 * j, 4, False)
            return c

        def pair_step(j, c):
            chunk(i, 4 * whole + 2 * j, 2, True)
            return c

        lax.fori_loop(0, whole, full_step, 0)
        lax.fori_loop(0, lax.div(rest, 2), pair_step, 0)

        @pl.when(lax.rem(rest, 2) == 1)
        def _():
            chunk(i, reached - 1, 1, True)

        return carry

    lax.fori_loop(0, NQ, query_block, 0)


def store_keys(dkv, refs):
    for n in range(NK):
        b, i = n // 2, n % 2
        ref = refs[b]
        rows = slice(i * BLK, (i + 1) * BLK)
        ref[rows, :BLK] = (dkv[n, :, :BLK] * SCALE).astype(ref.dtype)
        ref[rows, BLK:] = dkv[n, :, BLK:].astype(ref.dtype)


def first_kernel(meta, *refs):
    q_in, g_in, s_in, kv_in = refs[0:2], refs[2:4], refs[4:6], refs[6:10]
    q_all, g_all, qt, gt, stats, dqt = refs[10:16]
    dkv_out = refs[16]
    kv, kt, dkv, pieces, sems = refs[17:]
    copies = []
    for side in range(2):
        for i in range(2):
            rows = pl.ds(i * BLK, BLK)
            copies.append((q_in[side].at[rows], q_all.at[2 * side + i]))
            copies.append((g_in[side].at[rows], g_all.at[2 * side + i]))
        copies.append((s_in[side], pieces.at[side]))
    for b in range(4):
        source = kv_in[b].at[pl.ds(2 * BLK, 2 * BLK)]
        copies.append((source, kv.at[pl.ds(b * 2 * BLK, 2 * BLK)]))
    copies = [pltpu.make_async_copy(s, d, sems.at[n]) for n, (s, d) in enumerate(copies)]
    for copy in copies:
        copy.start()
    dqt[...] = jnp.zeros_like(dqt)
    for copy in copies:
        copy.wait()
    for side in range(2):
        stats[2 * side : 2 * side + 2, :] = pieces[side, 0:2, :]
        stats[NQ + 2 * side : NQ + 2 * side + 2, :] = pieces[side, 2:4, :]

    def transpose(n, carry):
        for h in range(H):
            cols = slice(h * BLK, (h + 1) * BLK)
            qt[n, :, cols] = q_all[n, :, cols].T
            gt[n, :, cols] = g_all[n, :, cols].T
        return carry

    lax.fori_loop(0, NQ, transpose, 0)
    for n in range(NK):
        kt[n] = kv[n * BLK : (n + 1) * BLK, :BLK].T
    key_steps(meta, q_all, g_all, qt, gt, stats, kv, kt, dqt, dkv)
    store_keys(dkv, [dkv_out.at[pl.ds(b * 2 * BLK, 2 * BLK)] for b in range(4)])


def second_kernel(meta, *refs):
    q_all, g_all, qt, gt, stats, dqt_in = refs[0:6]
    kv_in = refs[6:10]
    dq_own, dq_other = refs[10:12]
    dkv_out = refs[12:16]
    kv, kt, dkv, dqt, sems = refs[16:]
    copies = [
        pltpu.make_async_copy(
            kv_in[b].at[pl.ds(0, 2 * BLK)], kv.at[pl.ds(b * 2 * BLK, 2 * BLK)], sems.at[b]
        )
        for b in range(4)
    ]
    for copy in copies:
        copy.start()
    dqt[...] = dqt_in[...]
    for copy in copies:
        copy.wait()
    for n in range(NK):
        kt[n] = kv[n * BLK : (n + 1) * BLK, :BLK].T
    key_steps(meta, q_all, g_all, qt, gt, stats, kv, kt, dqt, dkv)
    store_keys(dkv, dkv_out)
    for n in range(NQ):
        ref = (dq_own, dq_own, dq_other, dq_other)[n]
        rows = slice(n % 2 * BLK, (n % 2 + 1) * BLK)
        for h in range(H):
            cols = slice(h * BLK, (h + 1) * BLK)
            ref[rows, cols] = (dqt[n, :, cols].T * SCALE).astype(ref.dtype)


WIDE = H * BLK
KEY_SCRATCH = [
    pltpu.VMEM((NK * BLK, 2 * BLK), BF16),
    pltpu.VMEM((NK, BLK, BLK), BF16),
    pltpu.VMEM((NK, BLK, 2 * BLK), F32),
]
COST = pl.CostEstimate(flops=10**10, bytes_accessed=2**20, transcendentals=2 * 10**6)


def first_call(meta, queries, grads, stats, blocks):
    rows = jax.ShapeDtypeStruct((NQ, BLK, WIDE), BF16)
    return pl.pallas_call(
        first_kernel,
        out_shape=(rows,) * 4
        + (
            jax.ShapeDtypeStruct((2 * NQ, WIDE), F32),
            jax.ShapeDtypeStruct((NQ, BLK, WIDE), F32),
        )
        + (jax.ShapeDtypeStruct((NK * BLK, 2 * BLK), BF16),),
        in_specs=[smem()] + [hbm(), anywhere()] * 2 + [anywhere()] * 6,
        out_specs=(vmem(),) * 7,
        scratch_shapes=KEY_SCRATCH
        + [pltpu.VMEM((2, 8, WIDE), F32), pltpu.SemaphoreType.DMA((14,))],
        compiler_params=pltpu.CompilerParams(vmem_limit_bytes=VMEM_LIMIT),
        cost_estimate=COST,
        name="attention_first",
    )(meta, *queries, *grads, *stats, *blocks)


def second_call(meta, carried, blocks):
    return pl.pallas_call(
        second_kernel,
        out_shape=(
            jax.ShapeDtypeStruct((256, WIDE), F32),
            jax.ShapeDtypeStruct((256, WIDE), BF16),
        )
        + (jax.ShapeDtypeStruct((2 * BLK, 2 * BLK), F32),) * 4,
        in_specs=[smem()] + [vmem()] * 6 + [anywhere()] * 4,
        out_specs=(vmem(),) * 6,
        scratch_shapes=KEY_SCRATCH
        + [pltpu.VMEM((NQ, BLK, WIDE), F32), pltpu.SemaphoreType.DMA((4,))],
        compiler_params=pltpu.CompilerParams(vmem_limit_bytes=VMEM_LIMIT),
        cost_estimate=COST,
        name="attention_second",
    )(meta, *carried, *blocks)


def make_meta(k_pos, q_pos):
    rank = jnp.sum(k_pos[None, :] < k_pos[:, None], axis=1)
    hit = rank[None, :] == jnp.arange(NK)[:, None]
    order = jnp.sum(jnp.where(hit, jnp.arange(NK)[None, :], 0), axis=1)
    ordered = jnp.sum(jnp.where(hit, k_pos[None, :], 0), axis=1)
    below = jnp.sum(k_pos[None, :] < q_pos[:, None], axis=1)
    reached = jnp.sum(k_pos[None, :] <= q_pos[:, None], axis=1)
    whole = below // 4
    return jnp.concatenate([order, ordered, q_pos, whole, reached]).astype(jnp.int32)


HALF = Z // 2


def project_kernel(a_ref, b_ref, c_ref, d_ref, ga, gb, gc, gd, out_ref):
    def step(j, carry):
        rows = pl.ds(pl.multiple_of(j * 512, 512), 512)
        terms = jnp.dot(a_ref[rows, :], ga[...], preferred_element_type=F32)
        terms = terms + jnp.dot(b_ref[rows, :], gb[...], preferred_element_type=F32)
        terms = terms + jnp.dot(c_ref[0, rows, :], gc[...], preferred_element_type=F32)
        terms = terms + jnp.dot(d_ref[rows, :], gd[...], preferred_element_type=F32)
        at = pl.ds(pl.multiple_of(j * 32, 32), 32)
        out_ref[:, at, :] = terms.astype(BF16).reshape(16, 32, 256)
        return carry

    lax.fori_loop(0, HALF, step, 0)


def project(turned, grads):
    return pl.pallas_call(
        project_kernel,
        out_shape=jax.ShapeDtypeStruct((16, HALF * 32, 256), BF16),
        in_specs=[vmem()] * 8,
        out_specs=vmem(),
        compiler_params=pltpu.CompilerParams(vmem_limit_bytes=12 * 2**20),
        cost_estimate=pl.CostEstimate(
            flops=2 * 4096 * 512 * 256, bytes_accessed=8 * 2**20, transcendentals=0
        ),
        name="project",
    )(*turned, *grads)


def sum_kernel(place, in_ref, own_ref, *out_refs):
    for k in range(HALF):
        at = pl.ds(pl.multiple_of((place[2] + k) % HALF * 32, 32), 32)
        value = in_ref[0, at, :].astype(F32)
        for j in range(1, 16):
            value = value + in_ref[j, at, :].astype(F32)
        ref = own_ref if k == 0 else out_refs[k - 1]
        ref[...] = value.astype(ref.dtype)


def sum_terms(place, terms):
    return pl.pallas_call(
        sum_kernel,
        out_shape=(jax.ShapeDtypeStruct((32, 256), F32),)
        + (jax.ShapeDtypeStruct((32, 256), BF16),) * (HALF - 1),
        in_specs=[smem(), vmem()],
        out_specs=(vmem(),) * HALF,
        compiler_params=pltpu.CompilerParams(vmem_limit_bytes=8 * 2**20),
        name="sum_terms",
    )(place, terms)


def body(layer_input, query_rows, key_rows, value_rows, attn_out, d_attn, log_sum_exp, block_order):
    z, x, yh, c = (lax.axis_index(name) for name in ("z", "x", "yh", "c"))
    ctx = (x * YH + yh) * C + c
    place = jnp.stack([c, z % 2, z // 2]).astype(jnp.int32)

    q, g = query_rows[0], d_attn[0]
    pair = jnp.concatenate([key_rows[0], value_rows[0]], axis=1)
    pair_y = fetch(pair, by_ctx(0, 1))
    q_other, g_other = fetch(q, swap_core), fetch(g, swap_core)
    stats = row_stats(attn_out[0], g, log_sum_exp[0])
    stats_other = fetch(stats, swap_core)
    both = jnp.concatenate([pair, pair_y], axis=0)
    blocks = [both] + [fetch(both, by_ctx(k, 0)) for k in ALONG_X[1:]]
    mine, other, away = turn(place, layer_input[0])

    places = block_order.reshape(16, 2)
    q_pos = jnp.concatenate([places[ctx], places[ctx ^ 1]])

    def owners(row):
        return jnp.concatenate([places[(x + k) % X * 4 + row * 2 + c] for k in ALONG_X])

    away = fetch(away, swap_z)
    mine_core = fetch(other, swap_core)
    blocks, mine = lax.optimization_barrier((blocks, mine))
    *carried, dkv_y = first_call(
        make_meta(owners(1 - yh), q_pos), (q, q_other), (g, g_other), (stats, stats_other), blocks
    )
    carried, mine_core = lax.optimization_barrier((carried, mine_core))
    carried, mine_core = lax.optimization_barrier((carried, mine_core))
    dq_own, dq_sent, *dkv = second_call(make_meta(owners(yh), q_pos), carried, blocks)
    dkv_y = fetch(dkv_y, by_ctx(0, 1))
    dkv = [part + dkv_y[256 * b : 256 * b + 256].astype(F32) for b, part in enumerate(dkv)]
    parts = [fetch(part.astype(BF16), by_ctx(-k, 0)) for k, part in zip(ALONG_X[1:], dkv[1:])]
    total = dkv[0]
    for part in parts:
        total = total + part.astype(F32)
    grads = total.astype(BF16)
    grads_z = fetch(grads, swap_z)
    grads_core = fetch(grads, swap_core)
    away, grads_zc = lax.optimization_barrier((away, fetch(grads_z, swap_core)))
    mine_zc = fetch(away[1], swap_core)

    terms = project((mine, mine_core, away, mine_zc), (grads, grads_core, grads_z, grads_zc))
    terms = lax.all_to_all(terms, ("yl", "x", "yh"), 0, 0)
    terms, dq_sent = lax.optimization_barrier((terms, dq_sent))
    own, *sent = sum_terms(place, terms)
    d_query = (dq_own + fetch(dq_sent, swap_core).astype(F32)).astype(BF16)[None]
    for k in range(1, HALF):
        own = own + fetch(sent[k - 1], by_z(-2 * k)).astype(F32)
    return (d_query, own)


def solution(mesh):
    fine = jax.sharding.Mesh(mesh.devices.reshape(Z, YL, X, YH, C), AXES)
    dp, ctx = ("z", "yl"), ("x", "yh", "c")
    rows = P(dp, ctx, None)
    return jax.shard_map(
        body,
        mesh=fine,
        in_specs=(rows, rows, rows, rows, rows, rows, P(dp, None, ctx), P()),
        out_specs=(rows, P(AXES, None)),
        check_vma=False,
    )
```

```python
import math

import jax
import jax.numpy as jnp
from jax import lax
from jax.experimental import pallas as pl
from jax.experimental.pallas import tpu as pltpu
from jax.sharding import PartitionSpec as P

F32 = jnp.float32
BF16 = jnp.bfloat16
BLK = 128
H = 8
Z, YL, X, YH, C = 8, 2, 4, 2, 2
AXES = ("z", "yl", "x", "yh", "c")
VMEM_LIMIT = 24 * 1024 * 1024


def coords(i):
    return (i // 32, i // 16 % 2, i // 4 % 4, i // 2 % 2, i % 2)


def index_of(z, yl, x, yh, c):
    return (((z * YL + yl) * X + x) * YH + yh) * C + c


def fetch(value, shift):
    pairs = [(index_of(*shift(*coords(i))), i) for i in range(Z * YL * X * YH * C)]
    return lax.ppermute(value, AXES, pairs)


def swap_core(z, yl, x, yh, c):
    return (z, yl, x, yh, 1 - c)


def by_ctx(dx, dyh):
    return lambda z, yl, x, yh, c: (z, yl, (x + dx) % X, yh ^ dyh, c)


def by_z(k):
    return lambda z, yl, x, yh, c: ((z + k) % Z, yl, x, yh, c)


def swap_z(z, yl, x, yh, c):
    return (z ^ 1, yl, x, yh, c)


ALONG_X = (0, 1, 3, 2)


def vmem():
    return pl.BlockSpec(memory_space=pltpu.VMEM)


def smem():
    return pl.BlockSpec(memory_space=pltpu.SMEM)


def anywhere():
    return pl.BlockSpec(memory_space=pl.ANY)


def hbm():
    return pl.BlockSpec(memory_space=pltpu.HBM)


def stats_kernel(out_hbm, grad_hbm, lse_hbm, stats_ref, out_ref, grad_ref, lse_ref, sems):
    pairs = ((out_hbm, out_ref), (grad_hbm, grad_ref), (lse_hbm, lse_ref))
    copies = [pltpu.make_async_copy(a, b, sems.at[n]) for n, (a, b) in enumerate(pairs)]
    for copy in copies:
        copy.start()
    stats_ref[4:8, :] = jnp.zeros((4, H * BLK), F32)
    for copy in copies:
        copy.wait()
    for h in range(H):
        cols = slice(h * BLK, (h + 1) * BLK)
        product = out_ref[:, cols].astype(F32) * grad_ref[:, cols].astype(F32)
        delta = jnp.sum(product.T, axis=0, keepdims=True)
        lse2 = lse_ref[h : h + 1, :] * math.log2(math.e)
        for i in range(2):
            rows = slice(i * BLK, (i + 1) * BLK)
            stats_ref[i : i + 1, cols] = lse2[:, rows]
            stats_ref[2 + i : 3 + i, cols] = delta[:, rows]


def row_stats(saved, grad, lse):
    return pl.pallas_call(
        stats_kernel,
        out_shape=jax.ShapeDtypeStruct((8, H * BLK), F32),
        in_specs=[hbm()] * 3,
        out_specs=vmem(),
        scratch_shapes=[
            pltpu.VMEM((256, H * BLK), BF16),
            pltpu.VMEM((256, H * BLK), BF16),
            pltpu.VMEM((H, 256), F32),
            pltpu.SemaphoreType.DMA((3,)),
        ],
        compiler_params=pltpu.CompilerParams(vmem_limit_bytes=8 * 2**20),
        cost_estimate=pl.CostEstimate(flops=10**6, bytes_accessed=2**20, transcendentals=0),
        name="row_stats",
    )(saved, grad, lse)


def turn_kernel(place, x_ref, mine_ref, other_ref, away_ref):
    even = place[0] == 0
    here = lax.rem(pl.program_id(0), 2) == place[1]
    half = pl.multiple_of(lax.div(pl.program_id(0), 2) * 512, 512)

    def cut(even_ref, odd_ref):
        for u in range(8):
            tile = x_ref[:, u * BLK : (u + 1) * BLK].T
            for yh in range(YH):
                at = pl.ds(half + (u * 64 + yh * 32), 32)
                even_ref[at, :] = tile[yh * 64 : yh * 64 + 32]
                odd_ref[at, :] = tile[yh * 64 + 32 : yh * 64 + 64]

    for holds, same, differs in (
        (here, mine_ref, other_ref),
        (jnp.logical_not(here), away_ref.at[0], away_ref.at[1]),
    ):

        @pl.when(jnp.logical_and(holds, even))
        def _():
            cut(same, differs)

        @pl.when(jnp.logical_and(holds, jnp.logical_not(even)))
        def _():
            cut(differs, same)


def turn(place, layer):
    half = jax.ShapeDtypeStruct((2048, 256), BF16)
    return pl.pallas_call(
        turn_kernel,
        grid=(Z,),
        out_shape=(half, half, jax.ShapeDtypeStruct((2, 2048, 256), BF16)),
        in_specs=[smem(), pl.BlockSpec((256, 1024), lambda z: (0, z))],
        out_specs=(
            pl.BlockSpec((2048, 256), lambda z: (0, 0)),
            pl.BlockSpec((2048, 256), lambda z: (0, 0)),
            pl.BlockSpec((2, 2048, 256), lambda z: (0, 0, 0)),
        ),
        compiler_params=pltpu.CompilerParams(vmem_limit_bytes=54 * 2**20),
        cost_estimate=pl.CostEstimate(flops=10**9, bytes_accessed=8 * 2**20, transcendentals=0),
        name="turn",
    )(place, layer)


NQ, NK = 4, 8
SCALE = BLK**-0.5


def key_steps(meta, q_all, g_all, qt, gt, stats, kv, kt, dqt, dkv):
    factor = SCALE * math.log2(math.e)
    dkv[...] = jnp.zeros_like(dkv)

    def chunk(i, first, count, masked):
        at = [meta[first + n] for n in range(count)]
        rows = [pl.ds(pl.multiple_of(a * BLK, BLK), BLK) for a in at]
        kb = jnp.concatenate([kv[r, :BLK] for r in rows], 0)
        vb = jnp.concatenate([kv[r, BLK:] for r in rows], 0)
        ktb = jnp.concatenate([kt[a] for a in at], 1)
        if masked:
            q_pos = meta[2 * NK + i]
            u = lax.broadcasted_iota(jnp.int32, (BLK, 2 * BLK), 0)
            t = lax.broadcasted_iota(jnp.int32, (BLK, 2 * BLK), 1) % BLK
            ahead = t - u
            visible = [ahead >= (meta[NK + first + n] - q_pos) * BLK for n in range(count)]
        def ahead_of(pair):
            cols = slice(pair * 2 * BLK, (pair + 1) * 2 * BLK)
            score = jnp.dot(kb, qt[i, :, cols], preferred_element_type=F32)
            return score, jnp.dot(vb, gt[i, :, cols], preferred_element_type=F32)

        probs, d_scores = [], []
        score, d_prob = ahead_of(0)
        for pair in range(H // 2):
            following = ahead_of(pair + 1) if pair + 1 < H // 2 else (None, None)
            cols = slice(pair * 2 * BLK, (pair + 1) * 2 * BLK)
            prob = jnp.exp2(score * factor - stats[pl.ds(i, 1), cols])
            if masked:
                prob = jnp.concatenate(
                    [
                        jnp.where(visible[n], prob[n * BLK : (n + 1) * BLK], 0.0)
                        for n in range(count)
                    ],
                    0,
                )
            d_scores.append((prob * (d_prob - stats[pl.ds(NQ + i, 1), cols])).astype(BF16))
            probs.append(prob.astype(BF16))
            score, d_prob = following
        prob = jnp.concatenate(probs, 1)
        d_score = jnp.concatenate(d_scores, 1)
        heads = [slice(h * BLK, (h + 1) * BLK) for h in range(H)]
        g_rows = jnp.concatenate([g_all[i, :, s] for s in heads], 0)
        q_rows = jnp.concatenate([q_all[i, :, s] for s in heads], 0)
        dv = jnp.dot(prob, g_rows, preferred_element_type=F32)
        dk = jnp.dot(d_score, q_rows, preferred_element_type=F32)
        dqt[i] += jnp.dot(ktb, d_score, preferred_element_type=F32)
        for n in range(count):
            dkv[at[n], :, :BLK] += dk[n * BLK : (n + 1) * BLK]
            dkv[at[n], :, BLK:] += dv[n * BLK : (n + 1) * BLK]

    def query_block(i, carry):
        whole = meta[2 * NK + NQ + i]
        reached = meta[2 * NK + 2 * NQ + i]
        rest = reached - 4 * whole

        def full_step(j, c):
            chunk(i, 4 * j, 4, False)
            return c

        def pair_step(j, c):
            chunk(i, 4 * whole + 2 * j, 2, True)
            return c

        lax.fori_loop(0, whole, full_step, 0)
        lax.fori_loop(0, lax.div(rest, 2), pair_step, 0)

        @pl.when(lax.rem(rest, 2) == 1)
        def _():
            chunk(i, reached - 1, 1, True)

        return carry

    lax.fori_loop(0, NQ, query_block, 0)


def store_keys(dkv, refs):
    for n in range(NK):
        b, i = n // 2, n % 2
        ref = refs[b]
        rows = slice(i * BLK, (i + 1) * BLK)
        ref[rows, :BLK] = (dkv[n, :, :BLK] * SCALE).astype(ref.dtype)
        ref[rows, BLK:] = dkv[n, :, BLK:].astype(ref.dtype)


def first_kernel(meta, *refs):
    q_in, g_in, s_in, kv_in = refs[0:2], refs[2:4], refs[4:6], refs[6:10]
    q_all, g_all, qt, gt, stats, dqt = refs[10:16]
    dkv_out = refs[16]
    kv, kt, dkv, pieces, sems = refs[17:]
    copies = []
    for side in range(2):
        for i in range(2):
            rows = pl.ds(i * BLK, BLK)
            copies.append((q_in[side].at[rows], q_all.at[2 * side + i]))
            copies.append((g_in[side].at[rows], g_all.at[2 * side + i]))
        copies.append((s_in[side], pieces.at[side]))
    for b in range(4):
        source = kv_in[b].at[pl.ds(2 * BLK, 2 * BLK)]
        copies.append((source, kv.at[pl.ds(b * 2 * BLK, 2 * BLK)]))
    copies = [pltpu.make_async_copy(s, d, sems.at[n]) for n, (s, d) in enumerate(copies)]
    for copy in copies:
        copy.start()
    dqt[...] = jnp.zeros_like(dqt)
    for copy in copies:
        copy.wait()
    for side in range(2):
        stats[2 * side : 2 * side + 2, :] = pieces[side, 0:2, :]
        stats[NQ + 2 * side : NQ + 2 * side + 2, :] = pieces[side, 2:4, :]

    def transpose(n, carry):
        for h in range(H):
            cols = slice(h * BLK, (h + 1) * BLK)
            qt[n, :, cols] = q_all[n, :, cols].T
            gt[n, :, cols] = g_all[n, :, cols].T
        return carry

    lax.fori_loop(0, NQ, transpose, 0)
    for n in range(NK):
        kt[n] = kv[n * BLK : (n + 1) * BLK, :BLK].T
    key_steps(meta, q_all, g_all, qt, gt, stats, kv, kt, dqt, dkv)
    store_keys(dkv, [dkv_out.at[pl.ds(b * 2 * BLK, 2 * BLK)] for b in range(4)])


def second_kernel(meta, *refs):
    q_all, g_all, qt, gt, stats, dqt_in = refs[0:6]
    kv_in = refs[6:10]
    dq_own, dq_other = refs[10:12]
    dkv_out = refs[12:16]
    kv, kt, dkv, dqt, sems = refs[16:]
    copies = [
        pltpu.make_async_copy(
            kv_in[b].at[pl.ds(0, 2 * BLK)], kv.at[pl.ds(b * 2 * BLK, 2 * BLK)], sems.at[b]
        )
        for b in range(4)
    ]
    for copy in copies:
        copy.start()
    dqt[...] = dqt_in[...]
    for copy in copies:
        copy.wait()
    for n in range(NK):
        kt[n] = kv[n * BLK : (n + 1) * BLK, :BLK].T
    key_steps(meta, q_all, g_all, qt, gt, stats, kv, kt, dqt, dkv)
    store_keys(dkv, dkv_out)
    for n in range(NQ):
        ref = (dq_own, dq_own, dq_other, dq_other)[n]
        rows = slice(n % 2 * BLK, (n % 2 + 1) * BLK)
        for h in range(H):
            cols = slice(h * BLK, (h + 1) * BLK)
            ref[rows, cols] = (dqt[n, :, cols].T * SCALE).astype(ref.dtype)


WIDE = H * BLK
KEY_SCRATCH = [
    pltpu.VMEM((NK * BLK, 2 * BLK), BF16),
    pltpu.VMEM((NK, BLK, BLK), BF16),
    pltpu.VMEM((NK, BLK, 2 * BLK), F32),
]
COST = pl.CostEstimate(flops=10**10, bytes_accessed=2**20, transcendentals=2 * 10**6)


def first_call(meta, queries, grads, stats, blocks):
    rows = jax.ShapeDtypeStruct((NQ, BLK, WIDE), BF16)
    return pl.pallas_call(
        first_kernel,
        out_shape=(rows,) * 4
        + (
            jax.ShapeDtypeStruct((2 * NQ, WIDE), F32),
            jax.ShapeDtypeStruct((NQ, BLK, WIDE), F32),
        )
        + (jax.ShapeDtypeStruct((NK * BLK, 2 * BLK), BF16),),
        in_specs=[smem()] + [hbm(), anywhere()] * 2 + [anywhere()] * 6,
        out_specs=(vmem(),) * 7,
        scratch_shapes=KEY_SCRATCH
        + [pltpu.VMEM((2, 8, WIDE), F32), pltpu.SemaphoreType.DMA((14,))],
        compiler_params=pltpu.CompilerParams(vmem_limit_bytes=VMEM_LIMIT),
        cost_estimate=COST,
        name="attention_first",
    )(meta, *queries, *grads, *stats, *blocks)


def second_call(meta, carried, blocks):
    return pl.pallas_call(
        second_kernel,
        out_shape=(
            jax.ShapeDtypeStruct((256, WIDE), F32),
            jax.ShapeDtypeStruct((256, WIDE), BF16),
        )
        + (jax.ShapeDtypeStruct((2 * BLK, 2 * BLK), F32),) * 4,
        in_specs=[smem()] + [vmem()] * 6 + [anywhere()] * 4,
        out_specs=(vmem(),) * 6,
        scratch_shapes=KEY_SCRATCH
        + [pltpu.VMEM((NQ, BLK, WIDE), F32), pltpu.SemaphoreType.DMA((4,))],
        compiler_params=pltpu.CompilerParams(vmem_limit_bytes=VMEM_LIMIT),
        cost_estimate=COST,
        name="attention_second",
    )(meta, *carried, *blocks)


def make_meta(k_pos, q_pos):
    rank = jnp.sum(k_pos[None, :] < k_pos[:, None], axis=1)
    hit = rank[None, :] == jnp.arange(NK)[:, None]
    order = jnp.sum(jnp.where(hit, jnp.arange(NK)[None, :], 0), axis=1)
    ordered = jnp.sum(jnp.where(hit, k_pos[None, :], 0), axis=1)
    below = jnp.sum(k_pos[None, :] < q_pos[:, None], axis=1)
    reached = jnp.sum(k_pos[None, :] <= q_pos[:, None], axis=1)
    whole = below // 4
    return jnp.concatenate([order, ordered, q_pos, whole, reached]).astype(jnp.int32)


HALF = Z // 2


def project_kernel(a_ref, b_ref, c_ref, d_ref, ga, gb, gc, gd, out_ref):
    def step(j, carry):
        rows = pl.ds(pl.multiple_of(j * 512, 512), 512)
        terms = jnp.dot(a_ref[rows, :], ga[...], preferred_element_type=F32)
        terms = terms + jnp.dot(b_ref[rows, :], gb[...], preferred_element_type=F32)
        terms = terms + jnp.dot(c_ref[0, rows, :], gc[...], preferred_element_type=F32)
        terms = terms + jnp.dot(d_ref[rows, :], gd[...], preferred_element_type=F32)
        at = pl.ds(pl.multiple_of(j * 32, 32), 32)
        out_ref[:, at, :] = terms.astype(BF16).reshape(16, 32, 256)
        return carry

    lax.fori_loop(0, HALF, step, 0)


def project(turned, grads):
    return pl.pallas_call(
        project_kernel,
        out_shape=jax.ShapeDtypeStruct((16, HALF * 32, 256), BF16),
        in_specs=[vmem()] * 8,
        out_specs=vmem(),
        compiler_params=pltpu.CompilerParams(vmem_limit_bytes=12 * 2**20),
        cost_estimate=pl.CostEstimate(
            flops=2 * 4096 * 512 * 256, bytes_accessed=8 * 2**20, transcendentals=0
        ),
        name="project",
    )(*turned, *grads)


def sum_kernel(place, in_ref, own_ref, *out_refs):
    for k in range(HALF):
        at = pl.ds(pl.multiple_of((place[2] + k) % HALF * 32, 32), 32)
        value = in_ref[0, at, :].astype(F32)
        for j in range(1, 16):
            value = value + in_ref[j, at, :].astype(F32)
        ref = own_ref if k == 0 else out_refs[k - 1]
        ref[...] = value.astype(ref.dtype)


def sum_terms(place, terms):
    return pl.pallas_call(
        sum_kernel,
        out_shape=(jax.ShapeDtypeStruct((32, 256), F32),)
        + (jax.ShapeDtypeStruct((32, 256), BF16),) * (HALF - 1),
        in_specs=[smem(), vmem()],
        out_specs=(vmem(),) * HALF,
        compiler_params=pltpu.CompilerParams(vmem_limit_bytes=8 * 2**20),
        name="sum_terms",
    )(place, terms)


def body(layer_input, query_rows, key_rows, value_rows, attn_out, d_attn, log_sum_exp, block_order):
    z, x, yh, c = (lax.axis_index(name) for name in ("z", "x", "yh", "c"))
    ctx = (x * YH + yh) * C + c
    place = jnp.stack([c, z % 2, z // 2]).astype(jnp.int32)

    q, g = query_rows[0], d_attn[0]
    pair = jnp.concatenate([key_rows[0], value_rows[0]], axis=1)
    pair_y = fetch(pair, by_ctx(0, 1))
    q_other, g_other = fetch(q, swap_core), fetch(g, swap_core)
    stats = row_stats(attn_out[0], g, log_sum_exp[0])
    stats_other = fetch(stats, swap_core)
    both = jnp.concatenate([pair, pair_y], axis=0)
    blocks = [both] + [fetch(both, by_ctx(k, 0)) for k in ALONG_X[1:]]
    mine, other, away = turn(place, layer_input[0])

    places = block_order.reshape(16, 2)
    q_pos = jnp.concatenate([places[ctx], places[ctx ^ 1]])

    def owners(row):
        return jnp.concatenate([places[(x + k) % X * 4 + row * 2 + c] for k in ALONG_X])

    away = fetch(away, swap_z)
    mine_core = fetch(other, swap_core)
    blocks, mine = lax.optimization_barrier((blocks, mine))
    *carried, dkv_y = first_call(
        make_meta(owners(1 - yh), q_pos), (q, q_other), (g, g_other), (stats, stats_other), blocks
    )
    carried, mine_core = lax.optimization_barrier((carried, mine_core))
    carried, mine_core = lax.optimization_barrier((carried, mine_core))
    dq_own, dq_sent, *dkv = second_call(make_meta(owners(yh), q_pos), carried, blocks)
    dkv_y = fetch(dkv_y, by_ctx(0, 1))
    dkv = [part + dkv_y[256 * b : 256 * b + 256].astype(F32) for b, part in enumerate(dkv)]
    parts = [fetch(part.astype(BF16), by_ctx(-k, 0)) for k, part in zip(ALONG_X[1:], dkv[1:])]
    total = dkv[0]
    for part in parts:
        total = total + part.astype(F32)
    grads = total.astype(BF16)
    grads_z = fetch(grads, swap_z)
    grads_core = fetch(grads, swap_core)
    away, grads_zc = lax.optimization_barrier((away, fetch(grads_z, swap_core)))
    mine_zc = fetch(away[1], swap_core)

    terms = project((mine, mine_core, away, mine_zc), (grads, grads_core, grads_z, grads_zc))
    terms = lax.all_to_all(terms, ("yl", "x", "yh"), 0, 0)
    terms, dq_sent = lax.optimization_barrier((terms, dq_sent))
    own, *sent = sum_terms(place, terms)
    d_query = (dq_own + fetch(dq_sent, swap_core).astype(F32)).astype(BF16)[None]
    for k in range(1, HALF):
        own = own + fetch(sent[k - 1], by_z(-2 * k)).astype(F32)
    return (d_query, own)


def solution(mesh):
    fine = jax.sharding.Mesh(mesh.devices.reshape(Z, YL, X, YH, C), AXES)
    dp, ctx = ("z", "yl"), ("x", "yh", "c")
    rows = P(dp, ctx, None)
    return jax.shard_map(
        body,
        mesh=fine,
        in_specs=(rows, rows, rows, rows, rows, rows, P(dp, None, ctx), P()),
        out_specs=(rows, P(AXES, None)),
        check_vma=False,
    )
```

```python
import math

import jax
import jax.numpy as jnp
from jax import lax
from jax.experimental import pallas as pl
from jax.experimental.pallas import tpu as pltpu
from jax.sharding import PartitionSpec as P

F32 = jnp.float32
BF16 = jnp.bfloat16
BLK = 128
H = 8
Z, YL, X, YH, C = 8, 2, 4, 2, 2
AXES = ("z", "yl", "x", "yh", "c")
VMEM_LIMIT = 24 * 1024 * 1024


def coords(i):
    return (i // 32, i // 16 % 2, i // 4 % 4, i // 2 % 2, i % 2)


def index_of(z, yl, x, yh, c):
    return (((z * YL + yl) * X + x) * YH + yh) * C + c


def fetch(value, shift):
    pairs = [(index_of(*shift(*coords(i))), i) for i in range(Z * YL * X * YH * C)]
    return lax.ppermute(value, AXES, pairs)


def swap_core(z, yl, x, yh, c):
    return (z, yl, x, yh, 1 - c)


def by_ctx(dx, dyh):
    return lambda z, yl, x, yh, c: (z, yl, (x + dx) % X, yh ^ dyh, c)


def by_z(k):
    return lambda z, yl, x, yh, c: ((z + k) % Z, yl, x, yh, c)


def swap_z(z, yl, x, yh, c):
    return (z ^ 1, yl, x, yh, c)


ALONG_X = (0, 1, 3, 2)


def vmem():
    return pl.BlockSpec(memory_space=pltpu.VMEM)


def smem():
    return pl.BlockSpec(memory_space=pltpu.SMEM)


def anywhere():
    return pl.BlockSpec(memory_space=pl.ANY)


def hbm():
    return pl.BlockSpec(memory_space=pltpu.HBM)


def stats_kernel(out_hbm, grad_hbm, lse_hbm, stats_ref, out_ref, grad_ref, lse_ref, sems):
    pairs = ((out_hbm, out_ref), (grad_hbm, grad_ref), (lse_hbm, lse_ref))
    copies = [pltpu.make_async_copy(a, b, sems.at[n]) for n, (a, b) in enumerate(pairs)]
    for copy in copies:
        copy.start()
    stats_ref[4:8, :] = jnp.zeros((4, H * BLK), F32)
    for copy in copies:
        copy.wait()
    for h in range(H):
        cols = slice(h * BLK, (h + 1) * BLK)
        product = out_ref[:, cols].astype(F32) * grad_ref[:, cols].astype(F32)
        delta = jnp.sum(product.T, axis=0, keepdims=True)
        lse2 = lse_ref[h : h + 1, :] * math.log2(math.e)
        for i in range(2):
            rows = slice(i * BLK, (i + 1) * BLK)
            stats_ref[i : i + 1, cols] = lse2[:, rows]
            stats_ref[2 + i : 3 + i, cols] = delta[:, rows]


def row_stats(saved, grad, lse):
    return pl.pallas_call(
        stats_kernel,
        out_shape=jax.ShapeDtypeStruct((8, H * BLK), F32),
        in_specs=[hbm()] * 3,
        out_specs=vmem(),
        scratch_shapes=[
            pltpu.VMEM((256, H * BLK), BF16),
            pltpu.VMEM((256, H * BLK), BF16),
            pltpu.VMEM((H, 256), F32),
            pltpu.SemaphoreType.DMA((3,)),
        ],
        compiler_params=pltpu.CompilerParams(vmem_limit_bytes=8 * 2**20),
        cost_estimate=pl.CostEstimate(flops=10**6, bytes_accessed=2**20, transcendentals=0),
        name="row_stats",
    )(saved, grad, lse)


def turn_kernel(place, x_ref, mine_ref, other_ref, away_ref):
    even = place[0] == 0
    here = lax.rem(pl.program_id(0), 2) == place[1]
    half = pl.multiple_of(lax.div(pl.program_id(0), 2) * 512, 512)

    def cut(even_ref, odd_ref):
        for u in range(8):
            tile = x_ref[:, u * BLK : (u + 1) * BLK].T
            for yh in range(YH):
                at = pl.ds(half + (u * 64 + yh * 32), 32)
                even_ref[at, :] = tile[yh * 64 : yh * 64 + 32]
                odd_ref[at, :] = tile[yh * 64 + 32 : yh * 64 + 64]

    for holds, same, differs in (
        (here, mine_ref, other_ref),
        (jnp.logical_not(here), away_ref.at[0], away_ref.at[1]),
    ):

        @pl.when(jnp.logical_and(holds, even))
        def _():
            cut(same, differs)

        @pl.when(jnp.logical_and(holds, jnp.logical_not(even)))
        def _():
            cut(differs, same)


def turn(place, layer):
    half = jax.ShapeDtypeStruct((2048, 256), BF16)
    return pl.pallas_call(
        turn_kernel,
        grid=(Z,),
        out_shape=(half, half, jax.ShapeDtypeStruct((2, 2048, 256), BF16)),
        in_specs=[smem(), pl.BlockSpec((256, 1024), lambda z: (0, z))],
        out_specs=(
            pl.BlockSpec((2048, 256), lambda z: (0, 0)),
            pl.BlockSpec((2048, 256), lambda z: (0, 0)),
            pl.BlockSpec((2, 2048, 256), lambda z: (0, 0, 0)),
        ),
        compiler_params=pltpu.CompilerParams(vmem_limit_bytes=54 * 2**20),
        cost_estimate=pl.CostEstimate(flops=10**9, bytes_accessed=8 * 2**20, transcendentals=0),
        name="turn",
    )(place, layer)


NQ, NK = 4, 8
SCALE = BLK**-0.5


def key_steps(meta, q_all, g_all, qt, gt, stats, kv, kt, dqt, dkv):
    factor = SCALE * math.log2(math.e)
    dkv[...] = jnp.zeros_like(dkv)

    def chunk(i, first, count, masked):
        at = [meta[first + n] for n in range(count)]
        rows = [pl.ds(pl.multiple_of(a * BLK, BLK), BLK) for a in at]
        kb = jnp.concatenate([kv[r, :BLK] for r in rows], 0)
        vb = jnp.concatenate([kv[r, BLK:] for r in rows], 0)
        ktb = jnp.concatenate([kt[a] for a in at], 1)
        if masked:
            q_pos = meta[2 * NK + i]
            u = lax.broadcasted_iota(jnp.int32, (BLK, 2 * BLK), 0)
            t = lax.broadcasted_iota(jnp.int32, (BLK, 2 * BLK), 1) % BLK
            ahead = t - u
            visible = [ahead >= (meta[NK + first + n] - q_pos) * BLK for n in range(count)]
        def ahead_of(pair):
            cols = slice(pair * 2 * BLK, (pair + 1) * 2 * BLK)
            score = jnp.dot(kb, qt[i, :, cols], preferred_element_type=F32)
            return score, jnp.dot(vb, gt[i, :, cols], preferred_element_type=F32)

        probs, d_scores = [], []
        score, d_prob = ahead_of(0)
        for pair in range(H // 2):
            following = ahead_of(pair + 1) if pair + 1 < H // 2 else (None, None)
            cols = slice(pair * 2 * BLK, (pair + 1) * 2 * BLK)
            prob = jnp.exp2(score * factor - stats[pl.ds(i, 1), cols])
            if masked:
                prob = jnp.concatenate(
                    [
                        jnp.where(visible[n], prob[n * BLK : (n + 1) * BLK], 0.0)
                        for n in range(count)
                    ],
                    0,
                )
            d_scores.append((prob * (d_prob - stats[pl.ds(NQ + i, 1), cols])).astype(BF16))
            probs.append(prob.astype(BF16))
            score, d_prob = following
        prob = jnp.concatenate(probs, 1)
        d_score = jnp.concatenate(d_scores, 1)
        heads = [slice(h * BLK, (h + 1) * BLK) for h in range(H)]
        g_rows = jnp.concatenate([g_all[i, :, s] for s in heads], 0)
        q_rows = jnp.concatenate([q_all[i, :, s] for s in heads], 0)
        dv = jnp.dot(prob, g_rows, preferred_element_type=F32)
        dk = jnp.dot(d_score, q_rows, preferred_element_type=F32)
        dqt[i] += jnp.dot(ktb, d_score, preferred_element_type=F32)
        for n in range(count):
            dkv[at[n], :, :BLK] += dk[n * BLK : (n + 1) * BLK]
            dkv[at[n], :, BLK:] += dv[n * BLK : (n + 1) * BLK]

    def query_block(i, carry):
        whole = meta[2 * NK + NQ + i]
        reached = meta[2 * NK + 2 * NQ + i]
        rest = reached - 4 * whole

        def full_step(j, c):
            chunk(i, 4 * j, 4, False)
            return c

        def pair_step(j, c):
            chunk(i, 4 * whole + 2 * j, 2, True)
            return c

        lax.fori_loop(0, whole, full_step, 0)
        lax.fori_loop(0, lax.div(rest, 2), pair_step, 0)

        @pl.when(lax.rem(rest, 2) == 1)
        def _():
            chunk(i, reached - 1, 1, True)

        return carry

    lax.fori_loop(0, NQ, query_block, 0)


def store_keys(dkv, refs):
    for n in range(NK):
        b, i = n // 2, n % 2
        ref = refs[b]
        rows = slice(i * BLK, (i + 1) * BLK)
        ref[rows, :BLK] = (dkv[n, :, :BLK] * SCALE).astype(ref.dtype)
        ref[rows, BLK:] = dkv[n, :, BLK:].astype(ref.dtype)


def first_kernel(meta, *refs):
    q_in, g_in, s_in, kv_in = refs[0:2], refs[2:4], refs[4:6], refs[6:10]
    q_all, g_all, qt, gt, stats, dqt = refs[10:16]
    dkv_out = refs[16]
    kv, kt, dkv, pieces, sems = refs[17:]
    copies = []
    for side in range(2):
        for i in range(2):
            rows = pl.ds(i * BLK, BLK)
            copies.append((q_in[side].at[rows], q_all.at[2 * side + i]))
            copies.append((g_in[side].at[rows], g_all.at[2 * side + i]))
        copies.append((s_in[side], pieces.at[side]))
    for b in range(4):
        source = kv_in[b].at[pl.ds(2 * BLK, 2 * BLK)]
        copies.append((source, kv.at[pl.ds(b * 2 * BLK, 2 * BLK)]))
    copies = [pltpu.make_async_copy(s, d, sems.at[n]) for n, (s, d) in enumerate(copies)]
    for copy in copies:
        copy.start()
    dqt[...] = jnp.zeros_like(dqt)
    for copy in copies:
        copy.wait()
    for side in range(2):
        stats[2 * side : 2 * side + 2, :] = pieces[side, 0:2, :]
        stats[NQ + 2 * side : NQ + 2 * side + 2, :] = pieces[side, 2:4, :]

    def transpose(n, carry):
        for h in range(H):
            cols = slice(h * BLK, (h + 1) * BLK)
            qt[n, :, cols] = q_all[n, :, cols].T
            gt[n, :, cols] = g_all[n, :, cols].T
        return carry

    lax.fori_loop(0, NQ, transpose, 0)
    for n in range(NK):
        kt[n] = kv[n * BLK : (n + 1) * BLK, :BLK].T
    key_steps(meta, q_all, g_all, qt, gt, stats, kv, kt, dqt, dkv)
    store_keys(dkv, [dkv_out.at[pl.ds(b * 2 * BLK, 2 * BLK)] for b in range(4)])


def second_kernel(meta, *refs):
    q_all, g_all, qt, gt, stats, dqt_in = refs[0:6]
    kv_in = refs[6:10]
    dq_own, dq_other = refs[10:12]
    dkv_out = refs[12:16]
    kv, kt, dkv, dqt, sems = refs[16:]
    copies = [
        pltpu.make_async_copy(
            kv_in[b].at[pl.ds(0, 2 * BLK)], kv.at[pl.ds(b * 2 * BLK, 2 * BLK)], sems.at[b]
        )
        for b in range(4)
    ]
    for copy in copies:
        copy.start()
    dqt[...] = dqt_in[...]
    for copy in copies:
        copy.wait()
    for n in range(NK):
        kt[n] = kv[n * BLK : (n + 1) * BLK, :BLK].T
    key_steps(meta, q_all, g_all, qt, gt, stats, kv, kt, dqt, dkv)
    store_keys(dkv, dkv_out)
    for n in range(NQ):
        ref = (dq_own, dq_own, dq_other, dq_other)[n]
        rows = slice(n % 2 * BLK, (n % 2 + 1) * BLK)
        for h in range(H):
            cols = slice(h * BLK, (h + 1) * BLK)
            ref[rows, cols] = (dqt[n, :, cols].T * SCALE).astype(ref.dtype)


WIDE = H * BLK
KEY_SCRATCH = [
    pltpu.VMEM((NK * BLK, 2 * BLK), BF16),
    pltpu.VMEM((NK, BLK, BLK), BF16),
    pltpu.VMEM((NK, BLK, 2 * BLK), F32),
]
COST = pl.CostEstimate(flops=10**10, bytes_accessed=2**20, transcendentals=2 * 10**6)


def first_call(meta, queries, grads, stats, blocks):
    rows = jax.ShapeDtypeStruct((NQ, BLK, WIDE), BF16)
    return pl.pallas_call(
        first_kernel,
        out_shape=(rows,) * 4
        + (
            jax.ShapeDtypeStruct((2 * NQ, WIDE), F32),
            jax.ShapeDtypeStruct((NQ, BLK, WIDE), F32),
        )
        + (jax.ShapeDtypeStruct((NK * BLK, 2 * BLK), BF16),),
        in_specs=[smem()] + [hbm(), anywhere()] * 2 + [anywhere()] * 6,
        out_specs=(vmem(),) * 7,
        scratch_shapes=KEY_SCRATCH
        + [pltpu.VMEM((2, 8, WIDE), F32), pltpu.SemaphoreType.DMA((14,))],
        compiler_params=pltpu.CompilerParams(vmem_limit_bytes=VMEM_LIMIT),
        cost_estimate=COST,
        name="attention_first",
    )(meta, *queries, *grads, *stats, *blocks)


def second_call(meta, carried, blocks):
    return pl.pallas_call(
        second_kernel,
        out_shape=(
            jax.ShapeDtypeStruct((256, WIDE), F32),
            jax.ShapeDtypeStruct((256, WIDE), BF16),
        )
        + (jax.ShapeDtypeStruct((2 * BLK, 2 * BLK), F32),) * 4,
        in_specs=[smem()] + [vmem()] * 6 + [anywhere()] * 4,
        out_specs=(vmem(),) * 6,
        scratch_shapes=KEY_SCRATCH
        + [pltpu.VMEM((NQ, BLK, WIDE), F32), pltpu.SemaphoreType.DMA((4,))],
        compiler_params=pltpu.CompilerParams(vmem_limit_bytes=VMEM_LIMIT),
        cost_estimate=COST,
        name="attention_second",
    )(meta, *carried, *blocks)


def make_meta(k_pos, q_pos):
    rank = jnp.sum(k_pos[None, :] < k_pos[:, None], axis=1)
    hit = rank[None, :] == jnp.arange(NK)[:, None]
    order = jnp.sum(jnp.where(hit, jnp.arange(NK)[None, :], 0), axis=1)
    ordered = jnp.sum(jnp.where(hit, k_pos[None, :], 0), axis=1)
    below = jnp.sum(k_pos[None, :] < q_pos[:, None], axis=1)
    reached = jnp.sum(k_pos[None, :] <= q_pos[:, None], axis=1)
    whole = below // 4
    return jnp.concatenate([order, ordered, q_pos, whole, reached]).astype(jnp.int32)


HALF = Z // 2


def project_kernel(a_ref, b_ref, c_ref, d_ref, ga, gb, gc, gd, out_ref):
    def step(j, carry):
        rows = pl.ds(pl.multiple_of(j * 512, 512), 512)
        terms = jnp.dot(a_ref[rows, :], ga[...], preferred_element_type=F32)
        terms = terms + jnp.dot(b_ref[rows, :], gb[...], preferred_element_type=F32)
        terms = terms + jnp.dot(c_ref[0, rows, :], gc[...], preferred_element_type=F32)
        terms = terms + jnp.dot(d_ref[rows, :], gd[...], preferred_element_type=F32)
        at = pl.ds(pl.multiple_of(j * 32, 32), 32)
        out_ref[:, at, :] = terms.astype(BF16).reshape(16, 32, 256)
        return carry

    lax.fori_loop(0, HALF, step, 0)


def project(turned, grads):
    return pl.pallas_call(
        project_kernel,
        out_shape=jax.ShapeDtypeStruct((16, HALF * 32, 256), BF16),
        in_specs=[vmem()] * 8,
        out_specs=vmem(),
        compiler_params=pltpu.CompilerParams(vmem_limit_bytes=12 * 2**20),
        cost_estimate=pl.CostEstimate(
            flops=2 * 4096 * 512 * 256, bytes_accessed=8 * 2**20, transcendentals=0
        ),
        name="project",
    )(*turned, *grads)


def sum_kernel(place, in_ref, own_ref, *out_refs):
    for k in range(HALF):
        at = pl.ds(pl.multiple_of((place[2] + k) % HALF * 32, 32), 32)
        value = in_ref[0, at, :].astype(F32)
        for j in range(1, 16):
            value = value + in_ref[j, at, :].astype(F32)
        ref = own_ref if k == 0 else out_refs[k - 1]
        ref[...] = value.astype(ref.dtype)


def sum_terms(place, terms):
    return pl.pallas_call(
        sum_kernel,
        out_shape=(jax.ShapeDtypeStruct((32, 256), F32),)
        + (jax.ShapeDtypeStruct((32, 256), BF16),) * (HALF - 1),
        in_specs=[smem(), vmem()],
        out_specs=(vmem(),) * HALF,
        compiler_params=pltpu.CompilerParams(vmem_limit_bytes=8 * 2**20),
        name="sum_terms",
    )(place, terms)


def body(layer_input, query_rows, key_rows, value_rows, attn_out, d_attn, log_sum_exp, block_order):
    z, x, yh, c = (lax.axis_index(name) for name in ("z", "x", "yh", "c"))
    ctx = (x * YH + yh) * C + c
    place = jnp.stack([c, z % 2, z // 2]).astype(jnp.int32)

    q, g = query_rows[0], d_attn[0]
    pair = jnp.concatenate([key_rows[0], value_rows[0]], axis=1)
    pair_y = fetch(pair, by_ctx(0, 1))
    q_other, g_other = fetch(q, swap_core), fetch(g, swap_core)
    stats = row_stats(attn_out[0], g, log_sum_exp[0])
    stats_other = fetch(stats, swap_core)
    both = jnp.concatenate([pair, pair_y], axis=0)
    blocks = [both] + [fetch(both, by_ctx(k, 0)) for k in ALONG_X[1:]]
    mine, other, away = turn(place, layer_input[0])

    places = block_order.reshape(16, 2)
    q_pos = jnp.concatenate([places[ctx], places[ctx ^ 1]])

    def owners(row):
        return jnp.concatenate([places[(x + k) % X * 4 + row * 2 + c] for k in ALONG_X])

    away = fetch(away, swap_z)
    blocks, mine, other = lax.optimization_barrier((blocks, mine, other))
    mine_core = fetch(other, swap_core)
    *carried, dkv_y = first_call(
        make_meta(owners(1 - yh), q_pos), (q, q_other), (g, g_other), (stats, stats_other), blocks
    )
    carried, mine_core = lax.optimization_barrier((carried, mine_core))
    carried, mine_core = lax.optimization_barrier((carried, mine_core))
    dq_own, dq_sent, *dkv = second_call(make_meta(owners(yh), q_pos), carried, blocks)
    dkv_y = fetch(dkv_y, by_ctx(0, 1))
    dkv = [part + dkv_y[256 * b : 256 * b + 256].astype(F32) for b, part in enumerate(dkv)]
    parts = [fetch(part.astype(BF16), by_ctx(-k, 0)) for k, part in zip(ALONG_X[1:], dkv[1:])]
    total = dkv[0]
    for part in parts:
        total = total + part.astype(F32)
    grads = total.astype(BF16)
    grads_z = fetch(grads, swap_z)
    grads_core = fetch(grads, swap_core)
    away, grads_zc = lax.optimization_barrier((away, fetch(grads_z, swap_core)))
    mine_zc = fetch(away[1], swap_core)

    terms = project((mine, mine_core, away, mine_zc), (grads, grads_core, grads_z, grads_zc))
    terms = lax.all_to_all(terms, ("yl", "x", "yh"), 0, 0)
    terms, dq_sent = lax.optimization_barrier((terms, dq_sent))
    own, *sent = sum_terms(place, terms)
    d_query = (dq_own + fetch(dq_sent, swap_core).astype(F32)).astype(BF16)[None]
    for k in range(1, HALF):
        own = own + fetch(sent[k - 1], by_z(-2 * k)).astype(F32)
    return (d_query, own)


def solution(mesh):
    fine = jax.sharding.Mesh(mesh.devices.reshape(Z, YL, X, YH, C), AXES)
    dp, ctx = ("z", "yl"), ("x", "yh", "c")
    rows = P(dp, ctx, None)
    return jax.shard_map(
        body,
        mesh=fine,
        in_specs=(rows, rows, rows, rows, rows, rows, P(dp, None, ctx), P()),
        out_specs=(rows, P(AXES, None)),
        check_vma=False,
    )
```
